256 devices in a mesh: pipe: 8 (over z), tensor: 4 (over x_hi, core), dp: 8 (over x_lo, y).
Axes of the slice: x: 4 (x_hi: 2, x_lo: 2; x = x_hi * 2 + x_lo), y: 4, z: 8, core: 2. Of those that a mesh axis runs over, the one named last changes fastest.
Arguments:
- norm_input: bfloat16 [8, 4, 512, 8192], P('pipe', None, 'dp', 'tensor'), may hold values from -256 to 256
- gain: float32 [8, 8192], P('pipe', 'tensor'), may hold values from 0.25 to 1.75
- value_weight: bfloat16 [8, 8192, 1024], P('pipe', 'tensor'), may hold values from -0.0625 to 0.0625
- shrink_factor_matrices: bfloat16 [8, 8, 8192, 64], P('pipe', None, 'tensor'), may hold values from -0.0625 to 0.0625
- expand_factor_matrices: bfloat16 [8, 8, 64, 1024], P('pipe'), may hold values from -0.1875 to 0.1875
- value_gradient: bfloat16 [8, 4, 512, 1024], P('pipe', None, 'dp'), may hold values from -6 to 6
- candidate_index: int32 [4, 32], P(None, 'dp'), may hold values from 0 to 7
- counts: int32 [8], replicated, may hold values from 128 to 512
Outputs:
- grad_in: bfloat16 [8, 4, 512, 8192], P('pipe', None, 'dp', 'tensor')
- grad_down: float32 [8, 8, 8192, 64], P('pipe', 'dp', 'tensor')
- grad_up: float32 [8, 8, 64, 1024], P('pipe', 'dp', None, 'tensor')
The draws below stay inside these ranges and needn't reach their ends.
All inputs are finite; a program needn't handle non-finite values.
Results may differ from the reference program's by a relative error of at most 0.0055.
Values sent between devices are 32-bit elements; how exact they have to be, the bound alone decides.
No kernel may reach another device: no remote copies, remote signals or barrier semaphores. Data moves between devices by JAX's collectives and lax.ppermute only.
A program may use at most 128 MiB of HBM per device.

```python
import math
import jax
import jax.numpy as jnp
from jax import lax

MODEL_WIDTH = 8192
VALUE_WIDTH = 1024
ADAPTER_RANK = 64
CANDIDATE_COUNT = 8
MB = 4
BLOCK_ROWS = 16
MICRO_TOKENS = 512
RELAY_SECTIONS = 8
N_PIPE = 8


def draw_norm_input(key, part):
    key = jax.random.fold_in(key, 7)
    key_base, key_rows, key_cols = jax.random.split(key, 3)
    shape = (N_PIPE, MB, MICRO_TOKENS, MODEL_WIDTH)
    row_scale = jnp.exp(jax.random.uniform(key_rows, (N_PIPE, MB, MICRO_TOKENS, 1), jnp.float32, 0.0, math.log(10.0)))
    col_scale = jnp.exp(jax.random.uniform(key_cols, (MODEL_WIDTH,), jnp.float32, 0.0, math.log(2.0)))
    col_scale = col_scale * jnp.exp(math.log(3.0) * jnp.arange(MODEL_WIDTH, dtype=jnp.float32) / MODEL_WIDTH)
    base = jnp.clip(jax.random.normal(key_base, shape, jnp.float32), -4.0, 4.0)
    return (0.5 * base * row_scale * col_scale).astype(jnp.bfloat16)


def touch_ends(result, own_key, least, top_value):
    shape = result.shape
    index_at = [jax.random.randint(jax.random.fold_in(own_key, axis), (), 0, shape[axis]) for axis in range(len(shape))]
    result = result.at[tuple(index_at)].set(least)
    longest = shape.index(max(shape))
    index_at[longest] = (index_at[longest] + 1) % shape[longest]
    return result.at[tuple(index_at)].set(top_value)


def shard_levels(key, shape, cuts, least, largest):
    level = 1.0
    for position, blocks in cuts:
        steps = jax.random.uniform(jax.random.fold_in(jax.random.fold_in(key, 6), position), (blocks,), jnp.float32, least / len(cuts), largest / len(cuts))
        level = level * jnp.repeat(jnp.exp(steps), shape[position] // blocks).reshape((-1,) + (1,) * (len(shape) - 1 - position))
    return level


def normal_values(rng, shape, scale, reach, cuts=(), kind=jnp.bfloat16):
    values = jax.random.normal(rng, shape, jnp.float32) * scale
    if len(cuts) > 0:
        values = shard_levels(rng, shape, cuts, -0.22, 0.18) * values
    return jnp.clip(values, min=-reach, max=reach).astype(kind)


def setup_inputs(seed: int = 0) -> dict:
    arg_keys = jax.random.split(jax.random.key(seed), 9)
    return {
        "norm_input": draw_norm_input(jax.random.fold_in(arg_keys[8], 71), 0),
        "gain": jnp.clip(1.0 + 0.15 * jax.random.normal(arg_keys[1], (RELAY_SECTIONS, MODEL_WIDTH), jnp.float32), 0.25, 1.75),
        "value_weight": normal_values(arg_keys[2], (RELAY_SECTIONS, MODEL_WIDTH, VALUE_WIDTH), MODEL_WIDTH ** -0.5, 0.0625, ((0, 8), (1, 4))),
        "shrink_factor_matrices": normal_values(arg_keys[3], (RELAY_SECTIONS, CANDIDATE_COUNT, MODEL_WIDTH, ADAPTER_RANK), MODEL_WIDTH ** -0.5, 0.0625, ((0, 8), (2, 4))),
        "expand_factor_matrices": normal_values(arg_keys[4], (RELAY_SECTIONS, CANDIDATE_COUNT, ADAPTER_RANK, VALUE_WIDTH), VALUE_WIDTH ** -0.5, 0.1875, ((0, 8),)),
        "value_gradient": normal_values(arg_keys[5], (RELAY_SECTIONS, MB, MICRO_TOKENS, VALUE_WIDTH), 1.0, 6.0, ((0, 8), (2, 8))),
        "candidate_index": touch_ends(jax.random.randint(arg_keys[6], (MB, MICRO_TOKENS // BLOCK_ROWS), 0, CANDIDATE_COUNT), jax.random.fold_in(arg_keys[6], 1), 0, CANDIDATE_COUNT - 1).astype(jnp.int32),
        "counts": touch_ends(jax.random.randint(arg_keys[7], (CANDIDATE_COUNT,), MB * MICRO_TOKENS // (2 * CANDIDATE_COUNT), 2 * MB * MICRO_TOKENS // CANDIDATE_COUNT + 1), jax.random.fold_in(arg_keys[7], 1), MB * MICRO_TOKENS // (2 * CANDIDATE_COUNT), (2 * MB * MICRO_TOKENS // CANDIDATE_COUNT + 1) - 1).astype(jnp.int32),
    }


adapter_scale = 2.0
eps = 1e-06

def one_micro(h_rows, gain_row, w_section, down_section, up_section, grad_rows, ids_row, weights):
    block_count = MICRO_TOKENS // BLOCK_ROWS
    cand = jnp.repeat(ids_row, BLOCK_ROWS)
    onehot = (cand[:, None] == jnp.arange(CANDIDATE_COUNT, dtype=jnp.int32)[None, :]).astype(jnp.float32)
    w_row = lax.optimization_barrier(jnp.sum(onehot * weights[None, :], axis=-1))
    multiplied_entries = (grad_rows.astype(jnp.float32) * w_row[:, None]).astype(jnp.bfloat16)
    h_full = h_rows.astype(jnp.float32)
    rms = jnp.sqrt(lax.optimization_barrier(jnp.mean(h_full * h_full, axis=-1, keepdims=True)) + eps)
    normed = (h_full * gain_row[None, :]).astype(jnp.bfloat16)
    down_per_block = down_section[ids_row].astype(jnp.float32)
    up_per_block = up_section[ids_row].astype(jnp.float32)
    normed_b = normed.astype(jnp.float32).reshape(block_count, BLOCK_ROWS, MODEL_WIDTH)
    scaled_up = multiplied_entries.astype(jnp.float32).reshape(block_count, BLOCK_ROWS, VALUE_WIDTH)
    rank_projected = jnp.einsum('nkd,ndr->nkr', normed_b, down_per_block).reshape(MICRO_TOKENS, ADAPTER_RANK)
    rank_projected = (rank_projected / rms).astype(jnp.bfloat16)
    backward_rank = jnp.einsum('iuc,iac->iua', scaled_up, up_per_block).reshape(MICRO_TOKENS, ADAPTER_RANK)
    backward_lowrank = backward_rank.astype(jnp.bfloat16)
    back_norm = (backward_rank / rms).astype(jnp.bfloat16)
    frozen_part = jnp.dot(multiplied_entries, w_section.T, preferred_element_type=jnp.float32)
    adapter_part = jnp.einsum('ghu,giu->ghi', backward_lowrank.astype(jnp.float32).reshape(block_count, BLOCK_ROWS, ADAPTER_RANK), down_per_block).reshape(MICRO_TOKENS, MODEL_WIDTH)
    normed_gradient = frozen_part + adapter_scale * adapter_part
    proj = lax.optimization_barrier(jnp.sum(h_full * gain_row[None, :] * normed_gradient, axis=-1, keepdims=True))
    contrib = gain_row[None, :] * normed_gradient / rms - h_full * proj / (MODEL_WIDTH * rms * rms * rms)
    block_onehot = (ids_row[:, None] == jnp.arange(CANDIDATE_COUNT, dtype=jnp.int32)[None, :]).astype(jnp.float32)
    tile_shrink_factor = jnp.einsum('nkd,nkr->ndr', normed_b, back_norm.astype(jnp.float32).reshape(block_count, BLOCK_ROWS, ADAPTER_RANK))
    down_gradient = adapter_scale * jnp.einsum('wp,wsy->psy', block_onehot, tile_shrink_factor)
    block_up_weight = jnp.einsum('wzp,wzq->wpq', rank_projected.astype(jnp.float32).reshape(block_count, BLOCK_ROWS, ADAPTER_RANK), scaled_up)
    up_gradient = adapter_scale * jnp.einsum('gy,gbo->ybo', block_onehot, block_up_weight)
    return (contrib, down_gradient, up_gradient)

def reference(norm_input, gain, value_weight, shrink_factor_matrices, expand_factor_matrices, value_gradient, candidate_index, counts):
    weights = MB * MICRO_TOKENS / (CANDIDATE_COUNT * counts.astype(jnp.float32))

    def relay_section(carry, items):
        h_section, gain_row, w_section, down_section, up_section, grad_section = items

        def micro(inputs):
            h_rows, grad_rows, ids_row = inputs
            return one_micro(h_rows, gain_row, w_section, down_section, up_section, grad_rows, ids_row, weights)
        contrib, down_gradient, up_gradient = lax.map(micro, (h_section, grad_section, candidate_index))
        carry = carry + contrib
        return (carry, (carry.astype(jnp.bfloat16), lax.optimization_barrier(jnp.sum(down_gradient, axis=0)), lax.optimization_barrier(jnp.sum(up_gradient, axis=0))))
    row_offset = jnp.zeros((MB, MICRO_TOKENS, MODEL_WIDTH), jnp.float32)
    ignored_carry, section_outputs = lax.scan(relay_section, row_offset, (norm_input, gain, value_weight, shrink_factor_matrices, expand_factor_matrices, value_gradient), reverse=True)
    grad_in, grad_down, grad_up = section_outputs
    return (grad_in, grad_down, grad_up)
```

```python
import functools

import jax
import jax.numpy as jnp
from jax import lax
from jax.experimental import pallas as pl
from jax.experimental.pallas import tpu as pltpu
from jax.sharding import PartitionSpec as P

MODEL_WIDTH = 8192
BLOCK_ROWS = 16
RANK = 64
ADAPTER_SCALE = 2.0
EPS = 1e-06
FIRST_BLOCK = 512
SECOND_BLOCK = 256
NT = (((1,), (1,)), ((), ()))
NN = (((1,), (0,)), ((), ()))
F32 = jnp.float32
BF16 = jnp.bfloat16


def dot(a, b, dims):
    return lax.dot_general(a, b, dims, preferred_element_type=F32)


def first_kernel(
    total_tokens,
    cand_ref,
    counts_ref,
    h_ref,
    gain_ref,
    weight_ref,
    shrink_ref,
    expand_ref,
    grad_ref,
    dn_ref,
    scaled_ref,
    back_ref,
    stat_ref,
    sel_ref,
    low_ref,
    sumsq_ref,
    proj_ref,
):
    step = pl.program_id(0)
    n_rows, n_sel = back_ref.shape
    n_blocks = n_rows // BLOCK_ROWS
    per_micro = cand_ref.shape[1]
    n_cand = counts_ref.shape[0]
    owner = lax.broadcasted_iota(jnp.int32, (BLOCK_ROWS, n_sel), 1) // RANK

    @pl.when(step == 0)
    def _():
        for block in range(n_blocks):
            cand = cand_ref[block // per_micro, block % per_micro]
            count = jnp.full((BLOCK_ROWS, 1), counts_ref[cand], jnp.int32).astype(F32)
            weight = total_tokens / (n_cand * count)
            rows = pl.ds(block * BLOCK_ROWS, BLOCK_ROWS)
            scaled_ref[rows, :] = (grad_ref[rows, :].astype(F32) * weight).astype(BF16)
        back = dot(scaled_ref[...], expand_ref[...], NT)
        for block in range(n_blocks):
            cand = cand_ref[block // per_micro, block % per_micro]
            rows = pl.ds(block * BLOCK_ROWS, BLOCK_ROWS)
            masked = jnp.where(
                owner == cand, back[block * BLOCK_ROWS : (block + 1) * BLOCK_ROWS], 0.0
            )
            back_ref[rows, :] = masked
            sel_ref[rows, :] = masked.astype(BF16)
        low_ref[...] = jnp.zeros_like(low_ref)
        sumsq_ref[...] = jnp.zeros_like(sumsq_ref)
        proj_ref[...] = jnp.zeros_like(proj_ref)

    h = h_ref[...].astype(F32)
    gained = h * gain_ref[...]
    shrink = shrink_ref[...]
    low_ref[...] += dot(gained.astype(BF16), shrink, NT)
    dn = dot(scaled_ref[...], weight_ref[...], NT) + ADAPTER_SCALE * dot(sel_ref[...], shrink, NN)
    dn_ref[...] = dn
    sumsq_ref[...] += jnp.sum(h * h, axis=1, keepdims=True)
    proj_ref[...] += jnp.sum(gained * dn, axis=1, keepdims=True)

    @pl.when(step == pl.num_programs(0) - 1)
    def _():
        lane = lax.broadcasted_iota(jnp.int32, (BLOCK_ROWS, 2 * RANK), 1)
        for block in range(n_blocks):
            cand = cand_ref[block // per_micro, block % per_micro]
            rows = pl.ds(block * BLOCK_ROWS, BLOCK_ROWS)
            masked = jnp.where(owner == cand, low_ref[rows, :], 0.0)
            folded = masked[:, : 2 * RANK]
            for part in range(1, n_sel // (2 * RANK)):
                folded += masked[:, part * 2 * RANK : (part + 1) * 2 * RANK]
            folded += pltpu.roll(folded, RANK, 1)
            stat_ref[rows, :] = jnp.where(
                lane < RANK,
                folded,
                jnp.where(
                    lane == RANK,
                    sumsq_ref[rows, :],
                    jnp.where(lane == RANK + 1, proj_ref[rows, :], 0.0),
                ),
            )


def second_kernel(
    cand_ref,
    here_ref,
    there_ref,
    dn_ref,
    h_ref,
    gain_ref,
    back_ref,
    scaled_ref,
    contrib_ref,
    adapter_ref,
    norm_sel_ref,
    low_sel_ref,
    inv_ref,
    proj_ref,
):
    step = pl.program_id(0)
    last = pl.num_programs(0) - 1
    n_rows, n_sel = back_ref.shape
    n_blocks = n_rows // BLOCK_ROWS
    per_micro = cand_ref.shape[1]

    @pl.when(step == 0)
    def _():
        stat = here_ref[...] + there_ref[...]
        rms = jnp.sqrt(stat[:, RANK : RANK + 1] / MODEL_WIDTH + EPS)
        inv_ref[...] = 1.0 / rms
        proj_ref[...] = stat[:, RANK + 1 : RANK + 2] / (MODEL_WIDTH * rms * rms * rms)
        norm_sel_ref[...] = (back_ref[...] / rms).T.astype(BF16)
        low = stat / rms
        lane = lax.broadcasted_iota(jnp.int32, (BLOCK_ROWS, 2 * RANK), 1)
        low = jnp.where(
            lax.broadcasted_iota(jnp.int32, (n_rows, 2 * RANK), 1) < RANK, low, 0.0
        )
        low = low + pltpu.roll(low, RANK, 1)
        pieces = []
        for block in range(n_blocks):
            cand = cand_ref[block // per_micro, block % per_micro]
            rows = low[block * BLOCK_ROWS : (block + 1) * BLOCK_ROWS]
            pieces.append(
                jnp.concatenate(
                    [
                        jnp.where(lane // RANK + 2 * part == cand, rows, 0.0)
                        for part in range(n_sel // (2 * RANK))
                    ],
                    axis=1,
                )
            )
        low_sel_ref[...] = jnp.concatenate(pieces, axis=0).T.astype(BF16)

    @pl.when(step < last)
    def _():
        h = h_ref[...].astype(F32)
        gained = h * gain_ref[...]
        contrib_ref[...] = gain_ref[...] * dn_ref[...] * inv_ref[...] - h * proj_ref[...]
        adapter_ref[...] = ADAPTER_SCALE * dot(norm_sel_ref[...], gained.astype(BF16), NN)

    @pl.when(step == last)
    def _():
        adapter_ref[...] = ADAPTER_SCALE * dot(low_sel_ref[...], scaled_ref[...], NN)


def body(
    norm_input,
    gain,
    value_weight,
    shrink_factor_matrices,
    expand_factor_matrices,
    value_gradient,
    candidate_index,
    counts,
):
    micro_count, tok_local, features = norm_input.shape[1:]
    n_rows = micro_count * tok_local
    n_cand = counts.shape[0]
    kv_width = value_weight.shape[2]
    n_tensor = lax.axis_size("tensor")
    n_pipe = lax.axis_size("pipe")
    kv_local = kv_width // n_tensor
    n_sel = n_cand * RANK
    total_tokens = float(n_rows * lax.axis_size("dp"))
    h = norm_input.reshape(n_rows, features)
    shrink = shrink_factor_matrices[0].transpose(0, 2, 1).reshape(n_sel, features)
    expand = expand_factor_matrices.reshape(n_sel, kv_width)
    gradient = value_gradient.reshape(n_rows, kv_width)

    smem = pl.BlockSpec(memory_space=pltpu.SMEM)

    def whole(shape):
        return pl.BlockSpec(shape, lambda i: (0, 0))

    params = pltpu.CompilerParams(
        dimension_semantics=("arbitrary",), vmem_limit_bytes=40 * 1024 * 1024
    )
    fb = FIRST_BLOCK
    dn, scaled, back, stat = pl.pallas_call(
        functools.partial(first_kernel, total_tokens),
        grid=(features // fb,),
        in_specs=[
            smem,
            smem,
            pl.BlockSpec((n_rows, fb), lambda i: (0, i)),
            pl.BlockSpec((1, fb), lambda i: (0, i)),
            pl.BlockSpec((fb, kv_width), lambda i: (i, 0)),
            pl.BlockSpec((n_sel, fb), lambda i: (0, i)),
            whole((n_sel, kv_width)),
            whole((n_rows, kv_width)),
        ],
        out_specs=[
            pl.BlockSpec((n_rows, fb), lambda i: (0, i)),
            whole((n_rows, kv_width)),
            whole((n_rows, n_sel)),
            whole((n_rows, 2 * RANK)),
        ],
        out_shape=[
            jax.ShapeDtypeStruct((n_rows, features), F32),
            jax.ShapeDtypeStruct((n_rows, kv_width), BF16),
            jax.ShapeDtypeStruct((n_rows, n_sel), F32),
            jax.ShapeDtypeStruct((n_rows, 2 * RANK), F32),
        ],
        scratch_shapes=[
            pltpu.VMEM((n_rows, n_sel), BF16),
            pltpu.VMEM((n_rows, n_sel), F32),
            pltpu.VMEM((n_rows, 1), F32),
            pltpu.VMEM((n_rows, 1), F32),
        ],
        compiler_params=params,
        name="first",
    )(
        candidate_index,
        counts,
        h,
        gain,
        value_weight[0],
        shrink,
        expand,
        gradient,
    )

    half = n_tensor // 2
    near = [(i, i ^ 1) for i in range(n_tensor)]
    far = [(i, (i + half) % n_tensor) for i in range(n_tensor)]
    here = stat + lax.ppermute(stat, "tensor", near)
    there = lax.ppermute(here, "tensor", far)

    scaled_part = lax.dynamic_slice_in_dim(
        scaled, lax.axis_index("tensor") * kv_local, kv_local, 1
    )
    sb = SECOND_BLOCK
    steps = features // sb

    def held(i):
        return (0, jnp.minimum(i, steps - 1))

    contrib, adapter = pl.pallas_call(
        second_kernel,
        grid=(steps + 1,),
        in_specs=[
            smem,
            whole((n_rows, 2 * RANK)),
            whole((n_rows, 2 * RANK)),
            pl.BlockSpec((n_rows, sb), held),
            pl.BlockSpec((n_rows, sb), held),
            pl.BlockSpec((1, sb), held),
            whole((n_rows, n_sel)),
            whole((n_rows, kv_local)),
        ],
        out_specs=[
            pl.BlockSpec((n_rows, sb), held),
            pl.BlockSpec((n_sel, sb), lambda i: (0, i)),
        ],
        out_shape=[
            jax.ShapeDtypeStruct((n_rows, features), F32),
            jax.ShapeDtypeStruct((n_sel, features + kv_local), F32),
        ],
        scratch_shapes=[
            pltpu.VMEM((n_sel, n_rows), BF16),
            pltpu.VMEM((n_sel, n_rows), BF16),
            pltpu.VMEM((n_rows, 1), F32),
            pltpu.VMEM((n_rows, 1), F32),
        ],
        compiler_params=params,
        name="second",
    )(candidate_index, here, there, dn, h, gain, back, scaled_part)

    adapter = lax.psum_scatter(
        adapter.reshape(n_cand, RANK, features + kv_local),
        "dp",
        scatter_dimension=0,
        tiled=True,
    )
    grad_down = adapter[:, :, :features].transpose(0, 2, 1)
    grad_up = adapter[:, :, features:]

    owned = lax.all_to_all(
        contrib.reshape(n_pipe, n_rows // n_pipe, features), "pipe", 0, 0, tiled=True
    )
    after = [jnp.zeros_like(owned[0])]
    for section in range(n_pipe - 1, 0, -1):
        after.append(after[-1] + owned[section])
    after = jnp.stack(after[::-1])
    behind = lax.all_to_all(after, "pipe", 0, 0, tiled=True).reshape(n_rows, features)
    grad_in = (contrib + behind).astype(BF16)
    return (
        grad_in.reshape(1, micro_count, tok_local, features),
        grad_down[None],
        grad_up[None],
    )


def solution(mesh):
    in_specs = (
        P("pipe", None, "dp", "tensor"),
        P("pipe", "tensor"),
        P("pipe", "tensor", None),
        P("pipe", None, "tensor", None),
        P("pipe", None, None, None),
        P("pipe", None, "dp", None),
        P(None, "dp"),
        P(),
    )
    out_specs = (
        P("pipe", None, "dp", "tensor"),
        P("pipe", "dp", "tensor", None),
        P("pipe", "dp", None, "tensor"),
    )
    return jax.shard_map(body, mesh=mesh, in_specs=in_specs, out_specs=out_specs, check_vma=False)
```

```python
import functools

import jax
import jax.numpy as jnp
from jax import lax
from jax.experimental import pallas as pl
from jax.experimental.pallas import tpu as pltpu
from jax.sharding import PartitionSpec as P

MODEL_WIDTH = 8192
BLOCK_ROWS = 16
RANK = 64
ADAPTER_SCALE = 2.0
EPS = 1e-06
FIRST_BLOCK = 512
PART_COLUMNS = (384, 1024)
VMEM_LIMIT = 16 * 1024 * 1024
FIRST_VMEM_LIMIT = 58 * 1024 * 1024
NT = (((1,), (1,)), ((), ()))
NN = (((1,), (0,)), ((), ()))
F32 = jnp.float32
BF16 = jnp.bfloat16


def dot(a, b, dims):
    return lax.dot_general(a, b, dims, preferred_element_type=F32)


def first_kernel(
    total_tokens,
    cand_hbm,
    counts_hbm,
    h_hbm,
    gain_hbm,
    weight_hbm,
    shrink_hbm,
    expand_hbm,
    grad_hbm,
    gained_dn_ref,
    normed_out,
    scaled_part_out,
    back_out,
    mask_out,
    stat_ref,
    normed_ref,
    scaled_part_ref,
    back_ref,
    mask_ref,
    cand_ref,
    counts_ref,
    h_ref,
    gain_ref,
    weight_ref,
    shrink_ref,
    expand_ref,
    grad_ref,
    scaled_ref,
    sel_ref,
    low_ref,
    sems,
    out_sems,
):
    n_rows, features = h_ref.shape
    n_sel = back_ref.shape[1]
    n_blocks = n_rows // BLOCK_ROWS
    per_micro = cand_ref.shape[1]
    n_cand = counts_ref.shape[0]
    kv_local = scaled_part_ref.shape[1]
    fb = FIRST_BLOCK
    n_steps = features // fb
    pairs = [
        (cand_hbm, cand_ref),
        (counts_hbm, counts_ref),
        (grad_hbm, grad_ref),
        (expand_hbm, expand_ref),
        (h_hbm, h_ref),
        (gain_hbm, gain_ref),
        (shrink_hbm, shrink_ref),
    ]
    copies = [
        pltpu.make_async_copy(source, target, sems.at[i]) for i, (source, target) in enumerate(pairs)
    ]
    for step in range(n_steps):
        rows = pl.ds(step * fb, fb)
        copies.append(
            pltpu.make_async_copy(
                weight_hbm.at[rows, :], weight_ref.at[rows, :], sems.at[len(pairs) + step]
            )
        )
    for copy in copies:
        copy.start()
    for copy in copies[:3]:
        copy.wait()

    leaving = []

    def leave(source, target):
        copy = pltpu.make_async_copy(source, target, out_sems.at[len(leaving)])
        copy.start()
        leaving.append(copy)

    owner = lax.broadcasted_iota(jnp.int32, (BLOCK_ROWS, n_sel), 1) // RANK
    for block in range(n_blocks):
        cand = cand_ref[block // per_micro, block % per_micro]
        count = jnp.full((BLOCK_ROWS, 1), counts_ref[cand], jnp.int32).astype(F32)
        weight = total_tokens / (n_cand * count)
        rows = pl.ds(block * BLOCK_ROWS, BLOCK_ROWS)
        scaled_ref[rows, :] = (grad_ref[rows, :].astype(F32) * weight).astype(BF16)
        mask_ref[rows, :] = jnp.where(owner == cand, 1.0, 0.0).astype(BF16)
    first_column = pl.multiple_of(lax.axis_index("tensor") * kv_local, kv_local)
    scaled_part_ref[...] = scaled_ref[:, pl.ds(first_column, kv_local)]
    leave(scaled_part_ref, scaled_part_out)
    leave(mask_ref, mask_out)
    copies[3].wait()
    back = dot(scaled_ref[...], expand_ref[...], NT) * mask_ref[...].astype(F32)
    back_ref[...] = back
    leave(back_ref, back_out)
    sel_ref[...] = back.astype(BF16)
    copies[4].wait()
    copies[5].wait()
    copies[6].wait()

    sumsq = jnp.zeros((n_rows, 1), F32)
    proj = jnp.zeros((n_rows, 1), F32)
    for step in range(n_steps):
        columns = pl.ds(step * fb, fb)
        h16 = h_ref[:, columns]
        h = h16.astype(F32)
        gain = gain_ref[:, columns]
        gained = h * gain
        normed = gained.astype(BF16)
        normed_ref[:, columns] = normed
        leave(normed_ref.at[:, columns], normed_out.at[:, columns])
        shrink = shrink_ref[:, columns]
        low = dot(normed, shrink, NT)
        if step == 0:
            low_ref[...] = low
        else:
            low_ref[...] += low
        sumsq += jnp.sum(h * h, axis=1, keepdims=True)
        adapter = dot(sel_ref[...], shrink, NN)
        copies[len(pairs) + step].wait()
        dn = dot(scaled_ref[...], weight_ref[columns, :], NT) + ADAPTER_SCALE * adapter
        gained_dn_ref[:, columns] = gain * dn
        proj += jnp.sum(gained * dn, axis=1, keepdims=True)

    masked = low_ref[...] * mask_ref[...].astype(F32)
    folded = masked[:, : 2 * RANK]
    for part in range(1, n_sel // (2 * RANK)):
        folded += masked[:, part * 2 * RANK : (part + 1) * 2 * RANK]
    folded += pltpu.roll(folded, RANK, 1)
    lane = lax.broadcasted_iota(jnp.int32, (n_rows, 2 * RANK), 1)
    stat_ref[...] = jnp.where(
        lane < RANK,
        folded,
        jnp.where(lane == RANK, sumsq, jnp.where(lane == RANK + 1, proj, 0.0)),
    )
    for copy in leaving:
        copy.wait()


def quarters():
    odd = lax.rem(lax.axis_index("pipe"), 2)
    return odd, (1 + 2 * odd, 2 - 2 * odd, odd, 3 - odd)


def rows_of(quarter, size):
    return pl.ds(pl.multiple_of(quarter * size, size), size)


def contrib_kernel(
    here_ref,
    there_ref,
    gained_dn_ref,
    h_hbm,
    up_ref,
    down_ref,
    first_ref,
    second_ref,
    h_ref,
    sems,
):
    size = up_ref.shape[0]
    order = quarters()[1]
    loads = []
    for i, quarter in enumerate(order):
        rows = rows_of(quarter, size)
        loads.append(pltpu.make_async_copy(h_hbm.at[rows, :], h_ref.at[rows, :], sems.at[i]))
    for copy in loads:
        copy.start()
    for i, target in enumerate((up_ref, down_ref, first_ref, second_ref)):
        rows = rows_of(order[i], size)
        stat = here_ref[rows, :] + there_ref[rows, :]
        rms = jnp.sqrt(stat[:, RANK : RANK + 1] / MODEL_WIDTH + EPS)
        inv = 1.0 / rms
        proj = stat[:, RANK + 1 : RANK + 2] / (MODEL_WIDTH * rms * rms * rms)
        loads[i].wait()
        target[...] = gained_dn_ref[rows, :] * inv - h_ref[rows, :].astype(F32) * proj


def pair_kernel(first_ref, second_ref, from_below_ref, from_above_ref, pair_ref):
    section = lax.axis_index("pipe")
    last = lax.axis_size("pipe") - 1
    odd = lax.rem(section, 2)
    owners, rows2, _ = pair_ref.shape
    rows = rows2 // 2
    for owner in range(owners):
        part = pl.ds(owner * rows, rows)
        below = from_below_ref[part, :]
        above = from_above_ref[part, :]
        pair_ref[owner, :rows, :] = first_ref[part, :] + jnp.where(odd == 1, below, above)
        mine = jnp.where(section == 0, 0.0, second_ref[part, :])
        other = jnp.where(odd == 1, above, below)
        pair_ref[owner, rows:, :] = mine + jnp.where(section == last, 0.0, other)


def scan_kernel(owned_ref, after_ref):
    groups, rows2, _ = owned_ref.shape
    rows = rows2 // 2
    total = jnp.zeros((rows, owned_ref.shape[2]), F32)
    for group in range(groups - 1, -1, -1):
        after_ref[group, :rows, :] = total
        if group:
            total = total + owned_ref[group, :rows, :]
    shift = 1 - lax.rem(lax.axis_index("pipe"), 2)
    places = [lax.rem(group + shift, groups) for group in range(groups)]
    total = owned_ref[places[groups - 1], rows:, :]
    for group in range(groups - 2, -1, -1):
        after_ref[places[group], rows:, :] = total
        total = total + owned_ref[places[group], rows:, :]
    after_ref[places[groups - 1], rows:, :] = total


def spread_kernel(after_ref, first_ref, second_ref, up_ref, down_ref):
    section = lax.axis_index("pipe")
    odd = lax.rem(section, 2)
    owners, rows2, _ = after_ref.shape
    rows = rows2 // 2
    for owner in range(owners):
        part = pl.ds(owner * rows, rows)
        after_first = after_ref[owner, :rows, :]
        after_second = after_ref[owner, rows:, :]
        up_ref[part, :] = jnp.where(odd == 1, after_second, after_first)
        down = jnp.where(
            odd == 1, after_first + first_ref[part, :], after_second + second_ref[part, :]
        )
        down_ref[part, :] = jnp.where(section == 0, 0.0, down)


def final_kernel(
    after_ref,
    up_ref,
    down_ref,
    first_ref,
    second_ref,
    from_below_ref,
    from_above_ref,
    last_below_ref,
    last_above_ref,
    out_ref,
):
    section = lax.axis_index("pipe")
    last = lax.axis_size("pipe") - 1
    odd, (up, down, first, second) = quarters()
    owners, rows2, _ = after_ref.shape
    rows = rows2 // 2
    size = owners * rows
    for owner in range(owners):
        part = pl.ds(owner * rows, rows)

        def place(quarter):
            return pl.ds(pl.multiple_of(quarter * size + owner * rows, rows), rows)

        above = from_above_ref[part, :]
        after = after_ref[owner, :rows, :] + jnp.where(odd == 1, 0.0, above)
        out_ref[place(first), :] = (after + first_ref[part, :]).astype(BF16)
        after = after_ref[owner, rows:, :] + jnp.where(odd == 1, above, 0.0)
        after = jnp.where(section == last, 0.0, after)
        out_ref[place(second), :] = (after + second_ref[part, :]).astype(BF16)
        out_ref[place(up), :] = (last_above_ref[part, :] + up_ref[part, :]).astype(BF16)
        out_ref[place(down), :] = (last_below_ref[part, :] + down_ref[part, :]).astype(BF16)


def adapter_kernel(
    here_ref,
    there_ref,
    back_ref,
    mask_ref,
    normed_ref,
    scaled_ref,
    *refs,
):
    *parts, norm_sel_ref, low_sel_ref = refs
    n_parts = len(parts) // 2
    n_rows, n_sel = back_ref.shape
    features = normed_ref.shape[1]
    half = n_sel // 2
    stat = here_ref[...] + there_ref[...]
    rms = jnp.sqrt(stat[:, RANK : RANK + 1] / MODEL_WIDTH + EPS)
    norm_sel_ref[...] = (back_ref[...] / rms).T.astype(BF16)
    lane = lax.broadcasted_iota(jnp.int32, (n_rows, 2 * RANK), 1)
    low = jnp.where(lane < RANK, stat / rms, 0.0)
    low = low + pltpu.roll(low, RANK, 1)
    low = jnp.concatenate([low] * (n_sel // (2 * RANK)), axis=1)
    low_sel_ref[...] = (low * mask_ref[...].astype(F32)).T.astype(BF16)
    mine = lax.axis_index("dp") // (lax.axis_size("dp") // 2)
    for targets, part in ((parts[:n_parts], mine), (parts[n_parts:], 1 - mine)):
        rows = rows_of(part, half)
        norm_sel = norm_sel_ref[rows, :]
        start = 0
        for target in targets:
            width = min(target.shape[1], features - start)
            for offset in range(0, width, FIRST_BLOCK):
                size = min(FIRST_BLOCK, width - offset)
                normed = normed_ref[:, start + offset : start + offset + size]
                target[:, offset : offset + size] = ADAPTER_SCALE * dot(norm_sel, normed, NN)
            start += width
            if width < target.shape[1]:
                target[:, width:] = ADAPTER_SCALE * dot(low_sel_ref[rows, :], scaled_ref[...], NN)


def split_kernel(keep_ref, come_ref, own_ref, *send_refs):
    parts = keep_ref.shape[0] // RANK
    mine = lax.rem(lax.axis_index("dp"), parts)
    for shift, target in enumerate((own_ref, *send_refs)):
        rows = rows_of(lax.rem(mine + shift, parts), RANK)
        target[...] = keep_ref[rows, :] + come_ref[rows, :]


def sum_kernel(*refs):
    total = refs[0][...]
    for ref in refs[1:-1]:
        total = total + ref[...]
    refs[-1][...] = total


def gather_kernel(*refs):
    *done, down_ref, up_ref = refs
    start = 0
    total = done[-4][...]
    for ref in done[-3:]:
        total = total + ref[...]
    for ref in done[:-4]:
        down_ref[:, start : start + ref.shape[1]] = ref[...]
        start += ref.shape[1]
    width = down_ref.shape[1] - start
    down_ref[:, start:] = total[:, :width]
    up_ref[...] = total[:, width:]


def call(kernel, name, outs, args, far=(), far_outs=(), scratch=(), limit=VMEM_LIMIT):
    def spec(place, places):
        return pl.BlockSpec(memory_space=pltpu.HBM if place in places else pltpu.VMEM)

    return pl.pallas_call(
        kernel,
        in_specs=[spec(i, far) for i in range(len(args))],
        out_specs=[spec(i, far_outs) for i in range(len(outs))],
        out_shape=[jax.ShapeDtypeStruct(shape, kind) for shape, kind in outs],
        scratch_shapes=list(scratch),
        compiler_params=pltpu.CompilerParams(vmem_limit_bytes=limit),
        name=name,
    )(*args)


def body(
    norm_input,
    gain,
    value_weight,
    shrink_factor_matrices,
    expand_factor_matrices,
    value_gradient,
    candidate_index,
    counts,
):
    micro_count, tok_local, features = norm_input.shape[1:]
    n_rows = micro_count * tok_local
    n_cand = counts.shape[0]
    kv_width = value_weight.shape[2]
    n_tensor = lax.axis_size("tensor")
    n_pipe = lax.axis_size("pipe")
    n_dp = lax.axis_size("dp")
    kv_local = kv_width // n_tensor
    n_sel = n_cand * RANK
    wide = features + kv_local
    total_tokens = float(n_rows * n_dp)
    h = norm_input.reshape(n_rows, features)
    shrink = shrink_factor_matrices[0].transpose(0, 2, 1).reshape(n_sel, features)
    expand = expand_factor_matrices.reshape(n_sel, kv_width)
    gradient = value_gradient.reshape(n_rows, kv_width)

    outs = [
        ((n_rows, features), F32),
        ((n_rows, features), BF16),
        ((n_rows, kv_local), BF16),
        ((n_rows, n_sel), F32),
        ((n_rows, n_sel), BF16),
        ((n_rows, 2 * RANK), F32),
    ]
    gained_dn, normed, scaled_part, back, mask, stat = call(
        functools.partial(first_kernel, total_tokens),
        "first",
        outs,
        (candidate_index, counts, h, gain, value_weight[0], shrink, expand, gradient),
        far=range(8),
        far_outs=range(1, 5),
        limit=FIRST_VMEM_LIMIT,
        scratch=[pltpu.VMEM(shape, kind) for shape, kind in outs[1:5]]
        + [
            pltpu.SMEM(candidate_index.shape, jnp.int32),
            pltpu.SMEM(counts.shape, jnp.int32),
            pltpu.VMEM((n_rows, features), BF16),
            pltpu.VMEM((1, features), F32),
            pltpu.VMEM((features, kv_width), BF16),
            pltpu.VMEM((n_sel, features), BF16),
            pltpu.VMEM((n_sel, kv_width), BF16),
            pltpu.VMEM((n_rows, kv_width), BF16),
            pltpu.VMEM((n_rows, kv_width), BF16),
            pltpu.VMEM((n_rows, n_sel), BF16),
            pltpu.VMEM((n_rows, n_sel), F32),
            pltpu.SemaphoreType.DMA((7 + features // FIRST_BLOCK,)),
            pltpu.SemaphoreType.DMA((3 + features // FIRST_BLOCK,)),
        ],
    )

    near = [(i, i ^ 1) for i in range(n_tensor)]
    far = [(i, (i + n_tensor // 2) % n_tensor) for i in range(n_tensor)]
    here = stat + lax.ppermute(stat, "tensor", near)
    there = lax.ppermute(here, "tensor", far)

    quarter = (n_rows // 4, features)
    up, down, first, second = call(
        contrib_kernel,
        "contrib",
        [(quarter, F32)] * 4,
        (here, there, gained_dn, h),
        far=(3,),
        scratch=[pltpu.VMEM((n_rows, features), BF16), pltpu.SemaphoreType.DMA((4,))],
    )
    rise = [(i, (i + 1) % n_pipe) for i in range(n_pipe)]
    fall = [(i, (i - 1) % n_pipe) for i in range(n_pipe)]
    from_below = lax.ppermute(up, "pipe", rise)
    from_above = lax.ppermute(down, "pipe", fall)

    half = n_sel // 2
    widths = (*PART_COLUMNS, wide - sum(PART_COLUMNS))
    n_parts = len(widths)
    adapter = call(
        adapter_kernel,
        "adapter",
        [((half, width), F32) for width in widths] * 2,
        (here, there, back, mask, normed, scaled_part),
        scratch=[pltpu.VMEM((n_sel, n_rows), BF16)] * 2,
    )
    keep, send = adapter[:n_parts], list(adapter[n_parts:])
    ring = n_dp // 2

    def across(part):
        pairs = [(i, (i + ring) % n_dp) for i in range(n_dp)]
        return lax.ppermute(send[part], "dp", pairs)

    def around(part, came):
        out = [((RANK, widths[part]), F32)] * ring
        own, *sends = call(split_kernel, "split", out, (keep[part], came))
        shares = [own]
        for shift, value in enumerate(sends, 1):
            pairs = [(i, i // ring * ring + (i + shift) % ring) for i in range(n_dp)]
            shares.append(lax.ppermute(value, "dp", pairs))
        return shares

    def summed(part, shares):
        return call(sum_kernel, "sum", [((RANK, widths[part]), F32)], shares)[0]

    groups = n_pipe // 2
    lines = [list(range(first, n_pipe, 2)) for first in range(2)]
    shape = (groups, n_rows // 2 // groups, features)
    came = across(0)
    from_below, from_above, came, *send[1:] = lax.optimization_barrier(
        (from_below, from_above, came, *send[1:])
    )
    (pair,) = call(pair_kernel, "pair", [(shape, F32)], (first, second, from_below, from_above))
    owned = lax.all_to_all(pair, "pipe", 0, 0, axis_index_groups=lines, tiled=True)
    part_0 = summed(0, around(0, came))
    came = across(1)
    owned, part_0, came, send[2] = lax.optimization_barrier((owned, part_0, came, send[2]))
    (after,) = call(scan_kernel, "scan", [(shape, F32)], (owned,))
    after = lax.all_to_all(after, "pipe", 0, 0, axis_index_groups=lines, tiled=True)
    part_1 = summed(1, around(1, came))
    came = across(2)
    after, part_1, came = lax.optimization_barrier((after, part_1, came))
    shares = around(2, came)
    rising, falling = call(spread_kernel, "spread", [(quarter, F32)] * 2, (after, first, second))
    last_below = lax.ppermute(rising, "pipe", rise)
    last_above = lax.ppermute(falling, "pipe", fall)
    grad_down, grad_up = call(
        gather_kernel, "gather", [((RANK, features), F32), ((RANK, kv_local), F32)], [part_0, part_1, *shares]
    )
    grad_down = grad_down.reshape(1, 1, RANK, features).transpose(0, 1, 3, 2)
    grad_up = grad_up.reshape(1, 1, RANK, kv_local)
    (grad_in,) = call(
        final_kernel,
        "final",
        [((n_rows, features), BF16)],
        (after, up, down, first, second, from_below, from_above, last_below, last_above),
    )
    return grad_in.reshape(1, micro_count, tok_local, features), grad_down, grad_up


def solution(mesh):
    in_specs = (
        P("pipe", None, "dp", "tensor"),
        P("pipe", "tensor"),
        P("pipe", "tensor", None),
        P("pipe", None, "tensor", None),
        P("pipe", None, None, None),
        P("pipe", None, "dp", None),
        P(None, "dp"),
        P(),
    )
    out_specs = (
        P("pipe", None, "dp", "tensor"),
        P("pipe", "dp", "tensor", None),
        P("pipe", "dp", None, "tensor"),
    )
    return jax.shard_map(body, mesh=mesh, in_specs=in_specs, out_specs=out_specs, check_vma=False)
```

```python
import functools

import jax
import jax.numpy as jnp
from jax import lax
from jax.experimental import pallas as pl
from jax.experimental.pallas import tpu as pltpu
from jax.sharding import PartitionSpec as P

MODEL_WIDTH = 8192
BLOCK_ROWS = 16
RANK = 64
ADAPTER_SCALE = 2.0
EPS = 1e-06
FIRST_BLOCK = 512
PART_COLUMNS = (256, 1024)
SWAP_COLUMNS = 384
VMEM_LIMIT = 16 * 1024 * 1024
FIRST_VMEM_LIMIT = 64 * 1024 * 1024
NT = (((1,), (1,)), ((), ()))
NN = (((1,), (0,)), ((), ()))
F32 = jnp.float32
BF16 = jnp.bfloat16


def dot(a, b, dims):
    return lax.dot_general(a, b, dims, preferred_element_type=F32)


def first_kernel(
    total_tokens,
    cand_hbm,
    counts_hbm,
    h_hbm,
    gain_hbm,
    weight_hbm,
    shrink_hbm,
    expand_hbm,
    grad_hbm,
    gained_dn_out,
    normed_out,
    scaled_part_out,
    back_out,
    mask_out,
    stat_out,
    gained_dn_ref,
    normed_ref,
    scaled_part_ref,
    back_ref,
    mask_ref,
    stat_ref,
    cand_ref,
    counts_ref,
    h_ref,
    gain_ref,
    weight_ref,
    shrink_ref,
    expand_ref,
    grad_ref,
    scaled_ref,
    sel_ref,
    low_ref,
    sems,
    out_sems,
):
    n_rows, features = h_ref.shape
    n_sel = back_ref.shape[1]
    n_blocks = n_rows // BLOCK_ROWS
    per_micro = cand_ref.shape[1]
    n_cand = counts_ref.shape[0]
    kv_local = scaled_part_ref.shape[1]
    fb = FIRST_BLOCK
    n_steps = features // fb
    pairs = [
        (cand_hbm, cand_ref),
        (counts_hbm, counts_ref),
        (grad_hbm, grad_ref),
        (expand_hbm, expand_ref),
        (h_hbm, h_ref),
        (gain_hbm, gain_ref),
        (shrink_hbm, shrink_ref),
    ]
    copies = [
        pltpu.make_async_copy(source, target, sems.at[i]) for i, (source, target) in enumerate(pairs)
    ]
    for step in range(n_steps):
        rows = pl.ds(step * fb, fb)
        copies.append(
            pltpu.make_async_copy(
                weight_hbm.at[rows, :], weight_ref.at[rows, :], sems.at[len(pairs) + step]
            )
        )
    for copy in copies:
        copy.start()
    for copy in copies[:3]:
        copy.wait()

    leaving = []

    def leave(source, target):
        copy = pltpu.make_async_copy(source, target, out_sems.at[len(leaving)])
        copy.start()
        leaving.append(copy)

    owner = lax.broadcasted_iota(jnp.int32, (BLOCK_ROWS, n_sel), 1) // RANK
    for block in range(n_blocks):
        cand = cand_ref[block // per_micro, block % per_micro]
        count = jnp.full((BLOCK_ROWS, 1), counts_ref[cand], jnp.int32).astype(F32)
        weight = total_tokens / (n_cand * count)
        rows = pl.ds(block * BLOCK_ROWS, BLOCK_ROWS)
        scaled_ref[rows, :] = (grad_ref[rows, :].astype(F32) * weight).astype(BF16)
        mask_ref[rows, :] = jnp.where(owner == cand, 1.0, 0.0).astype(BF16)
    first_column = pl.multiple_of(lax.axis_index("tensor") * kv_local, kv_local)
    scaled_part_ref[...] = scaled_ref[:, pl.ds(first_column, kv_local)]
    leave(scaled_part_ref, scaled_part_out)
    leave(mask_ref, mask_out)
    copies[3].wait()
    back = dot(scaled_ref[...], expand_ref[...], NT) * mask_ref[...].astype(F32)
    back_ref[...] = back
    leave(back_ref, back_out)
    sel_ref[...] = back.astype(BF16)
    copies[4].wait()
    copies[5].wait()
    copies[6].wait()

    sumsq = jnp.zeros((n_rows, 1), F32)
    proj = jnp.zeros((n_rows, 1), F32)
    for step in range(n_steps):
        columns = pl.ds(step * fb, fb)
        h16 = h_ref[:, columns]
        h = h16.astype(F32)
        gain = gain_ref[:, columns]
        gained = h * gain
        normed = gained.astype(BF16)
        normed_ref[:, columns] = normed
        leave(normed_ref.at[:, columns], normed_out.at[:, columns])
        shrink = shrink_ref[:, columns]
        low = dot(normed, shrink, NT)
        if step == 0:
            low_ref[...] = low
        else:
            low_ref[...] += low
        sumsq += jnp.sum(h * h, axis=1, keepdims=True)
        adapter = dot(sel_ref[...], shrink, NN)
        copies[len(pairs) + step].wait()
        dn = dot(scaled_ref[...], weight_ref[columns, :], NT) + ADAPTER_SCALE * adapter
        gained_dn_ref[:, columns] = gain * dn
        leave(gained_dn_ref.at[:, columns], gained_dn_out.at[:, columns])
        proj += jnp.sum(gained * dn, axis=1, keepdims=True)

    masked = low_ref[...] * mask_ref[...].astype(F32)
    folded = masked[:, : 2 * RANK]
    for part in range(1, n_sel // (2 * RANK)):
        folded += masked[:, part * 2 * RANK : (part + 1) * 2 * RANK]
    folded += pltpu.roll(folded, RANK, 1)
    lane = lax.broadcasted_iota(jnp.int32, (n_rows, 2 * RANK), 1)
    stat_ref[...] = jnp.where(
        lane < RANK,
        folded,
        jnp.where(lane == RANK, sumsq, jnp.where(lane == RANK + 1, proj, 0.0)),
    )
    leave(stat_ref, stat_out)
    for copy in leaving:
        copy.wait()


def quarters():
    odd = lax.rem(lax.axis_index("pipe"), 2)
    return odd, (1 + 2 * odd, 2 - 2 * odd, odd, 3 - odd)


def rows_of(quarter, size):
    return pl.ds(pl.multiple_of(quarter * size, size), size)


def contrib_kernel(
    here_ref,
    there_ref,
    gained_dn_ref,
    h_hbm,
    up_ref,
    down_ref,
    first_ref,
    second_ref,
    h_ref,
    sems,
):
    size = up_ref.shape[0]
    order = quarters()[1]
    loads = []
    for i, quarter in enumerate(order):
        rows = rows_of(quarter, size)
        loads.append(pltpu.make_async_copy(h_hbm.at[rows, :], h_ref.at[rows, :], sems.at[i]))
    for copy in loads:
        copy.start()
    for i, target in enumerate((up_ref, down_ref, first_ref, second_ref)):
        rows = rows_of(order[i], size)
        stat = here_ref[rows, :] + there_ref[rows, :]
        rms = jnp.sqrt(stat[:, RANK : RANK + 1] / MODEL_WIDTH + EPS)
        inv = 1.0 / rms
        proj = stat[:, RANK + 1 : RANK + 2] / (MODEL_WIDTH * rms * rms * rms)
        loads[i].wait()
        target[...] = gained_dn_ref[rows, :] * inv - h_ref[rows, :].astype(F32) * proj


def pair_kernel(first_ref, second_ref, from_below_ref, from_above_ref, pair_ref):
    section = lax.axis_index("pipe")
    last = lax.axis_size("pipe") - 1
    odd = lax.rem(section, 2)
    owners, rows2, _ = pair_ref.shape
    rows = rows2 // 2
    for owner in range(owners):
        part = pl.ds(owner * rows, rows)
        below = from_below_ref[part, :]
        above = from_above_ref[part, :]
        pair_ref[owner, :rows, :] = first_ref[part, :] + jnp.where(odd == 1, below, above)
        mine = jnp.where(section == 0, 0.0, second_ref[part, :])
        other = jnp.where(odd == 1, above, below)
        pair_ref[owner, rows:, :] = mine + jnp.where(section == last, 0.0, other)


def scan_kernel(owned_ref, after_ref):
    groups, rows2, _ = owned_ref.shape
    rows = rows2 // 2
    total = jnp.zeros((rows, owned_ref.shape[2]), F32)
    for group in range(groups - 1, -1, -1):
        after_ref[group, :rows, :] = total
        if group:
            total = total + owned_ref[group, :rows, :]
    shift = 1 - lax.rem(lax.axis_index("pipe"), 2)
    places = [lax.rem(group + shift, groups) for group in range(groups)]
    total = owned_ref[places[groups - 1], rows:, :]
    for group in range(groups - 2, -1, -1):
        after_ref[places[group], rows:, :] = total
        total = total + owned_ref[places[group], rows:, :]
    after_ref[places[groups - 1], rows:, :] = total


def spread_kernel(after_ref, first_ref, second_ref, up_ref, down_ref):
    section = lax.axis_index("pipe")
    odd = lax.rem(section, 2)
    owners, rows2, _ = after_ref.shape
    rows = rows2 // 2
    for owner in range(owners):
        part = pl.ds(owner * rows, rows)
        after_first = after_ref[owner, :rows, :]
        after_second = after_ref[owner, rows:, :]
        up_ref[part, :] = jnp.where(odd == 1, after_second, after_first)
        down = jnp.where(
            odd == 1, after_first + first_ref[part, :], after_second + second_ref[part, :]
        )
        down_ref[part, :] = jnp.where(section == 0, 0.0, down)


def final_kernel(
    after_ref,
    up_ref,
    down_ref,
    first_ref,
    second_ref,
    from_below_ref,
    from_above_ref,
    last_below_ref,
    last_above_ref,
    out_ref,
):
    section = lax.axis_index("pipe")
    last = lax.axis_size("pipe") - 1
    odd, (up, down, first, second) = quarters()
    owners, rows2, _ = after_ref.shape
    rows = rows2 // 2
    size = owners * rows
    for owner in range(owners):
        part = pl.ds(owner * rows, rows)

        def place(quarter):
            return pl.ds(pl.multiple_of(quarter * size + owner * rows, rows), rows)

        above = from_above_ref[part, :]
        after = after_ref[owner, :rows, :] + jnp.where(odd == 1, 0.0, above)
        out_ref[place(first), :] = (after + first_ref[part, :]).astype(BF16)
        after = after_ref[owner, rows:, :] + jnp.where(odd == 1, above, 0.0)
        after = jnp.where(section == last, 0.0, after)
        out_ref[place(second), :] = (after + second_ref[part, :]).astype(BF16)
        out_ref[place(up), :] = (last_above_ref[part, :] + up_ref[part, :]).astype(BF16)
        out_ref[place(down), :] = (last_below_ref[part, :] + down_ref[part, :]).astype(BF16)


def adapter_kernel(
    here_ref,
    there_ref,
    back_ref,
    mask_ref,
    normed_ref,
    scaled_ref,
    *refs,
):
    *parts, norm_sel_ref, low_sel_ref = refs
    n_parts = len(PART_COLUMNS) + 1
    swaps = parts[2 * n_parts :]
    ring = len(swaps)
    n_rows, n_sel = back_ref.shape
    features = normed_ref.shape[1]
    half = n_sel // 2
    stat = here_ref[...] + there_ref[...]
    rms = jnp.sqrt(stat[:, RANK : RANK + 1] / MODEL_WIDTH + EPS)
    norm_sel_ref[...] = (back_ref[...] / rms).T.astype(BF16)
    lane = lax.broadcasted_iota(jnp.int32, (n_rows, 2 * RANK), 1)
    low = jnp.where(lane < RANK, stat / rms, 0.0)
    low = low + pltpu.roll(low, RANK, 1)
    low = jnp.concatenate([low] * (n_sel // (2 * RANK)), axis=1)
    low_sel_ref[...] = (low * mask_ref[...].astype(F32)).T.astype(BF16)
    mine = lax.axis_index("dp") // ring
    for targets, part in ((parts[n_parts : 2 * n_parts], 1 - mine), (parts[:n_parts], mine)):
        rows = rows_of(part, half)
        norm_sel = norm_sel_ref[rows, :]
        start = 0
        for i, target in enumerate(targets):
            if i == n_parts - 1:
                start += SWAP_COLUMNS
            width = min(target.shape[1], features - start)
            for offset in range(0, width, FIRST_BLOCK):
                size = min(FIRST_BLOCK, width - offset)
                normed = normed_ref[:, start + offset : start + offset + size]
                target[:, offset : offset + size] = ADAPTER_SCALE * dot(norm_sel, normed, NN)
            start += width
            if width < target.shape[1]:
                target[:, width:] = ADAPTER_SCALE * dot(low_sel_ref[rows, :], scaled_ref[...], NN)
    start = sum(PART_COLUMNS)
    normed = normed_ref[:, start : start + SWAP_COLUMNS]
    mine = lax.rem(lax.axis_index("dp"), ring)
    for shift, target in enumerate(swaps):
        owner = lax.rem(mine + shift, ring)
        for upper in range(2):
            norm_sel = norm_sel_ref[rows_of(upper * ring + owner, RANK), :]
            target[upper * RANK : (upper + 1) * RANK, :] = ADAPTER_SCALE * dot(norm_sel, normed, NN)


def split_kernel(keep_ref, come_ref, own_ref, *send_refs):
    parts = keep_ref.shape[0] // RANK
    mine = lax.rem(lax.axis_index("dp"), parts)
    for shift, target in enumerate((own_ref, *send_refs)):
        rows = rows_of(lax.rem(mine + shift, parts), RANK)
        target[...] = keep_ref[rows, :] + come_ref[rows, :]


def sum_kernel(*refs):
    total = refs[0][...]
    for ref in refs[1:-1]:
        total = total + ref[...]
    refs[-1][...] = total


def swap_kernel(*refs):
    *shares, keep_ref, send_ref, total_ref = refs
    total = shares[0][...]
    for ref in shares[1:]:
        total = total + ref[...]
    total_ref[...] = total
    mine = lax.axis_index("dp") // len(shares)
    keep_ref[...] = total_ref[rows_of(mine, RANK), :]
    send_ref[...] = total_ref[rows_of(1 - mine, RANK), :]


def gather_kernel(part_0_ref, part_1_ref, swap_keep_ref, swap_come_ref, *refs):
    *shares, down_ref, up_ref = refs
    total = shares[0][...]
    for ref in shares[1:]:
        total = total + ref[...]
    start = 0
    for value in (part_0_ref[...], part_1_ref[...], swap_keep_ref[...] + swap_come_ref[...]):
        down_ref[:, start : start + value.shape[1]] = value
        start += value.shape[1]
    width = down_ref.shape[1] - start
    down_ref[:, start:] = total[:, :width]
    up_ref[...] = total[:, width:]


def call(kernel, name, outs, args, far=(), far_outs=(), scratch=(), limit=VMEM_LIMIT):
    def spec(place, places):
        return pl.BlockSpec(memory_space=pltpu.HBM if place in places else pltpu.VMEM)

    return pl.pallas_call(
        kernel,
        in_specs=[spec(i, far) for i in range(len(args))],
        out_specs=[spec(i, far_outs) for i in range(len(outs))],
        out_shape=[jax.ShapeDtypeStruct(shape, kind) for shape, kind in outs],
        scratch_shapes=list(scratch),
        compiler_params=pltpu.CompilerParams(vmem_limit_bytes=limit),
        name=name,
    )(*args)


def body(
    norm_input,
    gain,
    value_weight,
    shrink_factor_matrices,
    expand_factor_matrices,
    value_gradient,
    candidate_index,
    counts,
):
    micro_count, tok_local, features = norm_input.shape[1:]
    n_rows = micro_count * tok_local
    n_cand = counts.shape[0]
    kv_width = value_weight.shape[2]
    n_tensor = lax.axis_size("tensor")
    n_pipe = lax.axis_size("pipe")
    n_dp = lax.axis_size("dp")
    kv_local = kv_width // n_tensor
    n_sel = n_cand * RANK
    wide = features + kv_local
    total_tokens = float(n_rows * n_dp)
    h = norm_input.reshape(n_rows, features)
    shrink = shrink_factor_matrices[0].transpose(0, 2, 1).reshape(n_sel, features)
    expand = expand_factor_matrices.reshape(n_sel, kv_width)
    gradient = value_gradient.reshape(n_rows, kv_width)

    outs = [
        ((n_rows, features), F32),
        ((n_rows, features), BF16),
        ((n_rows, kv_local), BF16),
        ((n_rows, n_sel), F32),
        ((n_rows, n_sel), BF16),
        ((n_rows, 2 * RANK), F32),
    ]
    gained_dn, normed, scaled_part, back, mask, stat = call(
        functools.partial(first_kernel, total_tokens),
        "first",
        outs,
        (candidate_index, counts, h, gain, value_weight[0], shrink, expand, gradient),
        far=range(8),
        far_outs=range(6),
        limit=FIRST_VMEM_LIMIT,
        scratch=[pltpu.VMEM(shape, kind) for shape, kind in outs]
        + [
            pltpu.SMEM(candidate_index.shape, jnp.int32),
            pltpu.SMEM(counts.shape, jnp.int32),
            pltpu.VMEM((n_rows, features), BF16),
            pltpu.VMEM((1, features), F32),
            pltpu.VMEM((features, kv_width), BF16),
            pltpu.VMEM((n_sel, features), BF16),
            pltpu.VMEM((n_sel, kv_width), BF16),
            pltpu.VMEM((n_rows, kv_width), BF16),
            pltpu.VMEM((n_rows, kv_width), BF16),
            pltpu.VMEM((n_rows, n_sel), BF16),
            pltpu.VMEM((n_rows, n_sel), F32),
            pltpu.SemaphoreType.DMA((7 + features // FIRST_BLOCK,)),
            pltpu.SemaphoreType.DMA((4 + 2 * (features // FIRST_BLOCK),)),
        ],
    )

    near = [(i, i ^ 1) for i in range(n_tensor)]
    far = [(i, (i + n_tensor // 2) % n_tensor) for i in range(n_tensor)]
    here = stat + lax.ppermute(stat, "tensor", near)
    there = lax.ppermute(here, "tensor", far)

    quarter = (n_rows // 4, features)
    up, down, first, second = call(
        contrib_kernel,
        "contrib",
        [(quarter, F32)] * 4,
        (here, there, gained_dn, h),
        far=(3,),
        scratch=[pltpu.VMEM((n_rows, features), BF16), pltpu.SemaphoreType.DMA((4,))],
    )
    rise = [(i, (i + 1) % n_pipe) for i in range(n_pipe)]
    fall = [(i, (i - 1) % n_pipe) for i in range(n_pipe)]
    from_below = lax.ppermute(up, "pipe", rise)
    from_above = lax.ppermute(down, "pipe", fall)

    half = n_sel // 2
    ring = n_dp // 2
    widths = (*PART_COLUMNS, wide - sum(PART_COLUMNS) - SWAP_COLUMNS)
    n_parts = len(widths)
    adapter = call(
        adapter_kernel,
        "adapter",
        [((half, width), F32) for width in widths] * 2 + [((2 * RANK, SWAP_COLUMNS), F32)] * ring,
        (here, there, back, mask, normed, scaled_part),
        scratch=[pltpu.VMEM((n_sel, n_rows), BF16)] * 2,
    )
    keep, send = adapter[:n_parts], list(adapter[n_parts : 2 * n_parts])
    swaps = adapter[2 * n_parts :]

    def over(value):
        pairs = [(i, (i + ring) % n_dp) for i in range(n_dp)]
        return lax.ppermute(value, "dp", pairs)

    def across(part):
        return over(send[part])

    def around(part, came):
        out = [((RANK, widths[part]), F32)] * ring
        return turned(call(split_kernel, "split", out, (keep[part], came)))

    def turned(values):
        own, *sends = values
        shares = [own]
        for shift, value in enumerate(sends, 1):
            pairs = [(i, i // ring * ring + (i + shift) % ring) for i in range(n_dp)]
            shares.append(lax.ppermute(value, "dp", pairs))
        return shares

    def summed(part, shares):
        return call(sum_kernel, "sum", [((RANK, widths[part]), F32)], shares)[0]

    groups = n_pipe // 2
    lines = [list(range(first, n_pipe, 2)) for first in range(2)]
    shape = (groups, n_rows // 2 // groups, features)
    came = across(0)
    from_below, from_above, came, send[1], send[2], *swaps = lax.optimization_barrier(
        (from_below, from_above, came, send[1], send[2], *swaps)
    )
    (pair,) = call(pair_kernel, "pair", [(shape, F32)], (first, second, from_below, from_above))
    owned = lax.all_to_all(pair, "pipe", 0, 0, axis_index_groups=lines, tiled=True)
    part_0 = summed(0, around(0, came))
    came = across(1)
    swap_keep, swap_send = call(
        swap_kernel,
        "swap",
        [((RANK, SWAP_COLUMNS), F32)] * 2,
        turned(swaps),
        scratch=[pltpu.VMEM((2 * RANK, SWAP_COLUMNS), F32)],
    )
    owned, part_0, came, send[2], swap_send = lax.optimization_barrier(
        (owned, part_0, came, send[2], swap_send)
    )
    (after,) = call(scan_kernel, "scan", [(shape, F32)], (owned,))
    after = lax.all_to_all(after, "pipe", 0, 0, axis_index_groups=lines, tiled=True)
    part_1 = summed(1, around(1, came))
    came = across(2)
    swap_come = over(swap_send)
    after, part_1, came, swap_come = lax.optimization_barrier((after, part_1, came, swap_come))
    shares = around(2, came)
    rising, falling = call(spread_kernel, "spread", [(quarter, F32)] * 2, (after, first, second))
    last_below = lax.ppermute(rising, "pipe", rise)
    last_above = lax.ppermute(falling, "pipe", fall)
    grad_down, grad_up = call(
        gather_kernel, "gather", [((RANK, features), F32), ((RANK, kv_local), F32)], [part_0, part_1, swap_keep, swap_come, *shares]
    )
    grad_down = grad_down.reshape(1, 1, RANK, features).transpose(0, 1, 3, 2)
    grad_up = grad_up.reshape(1, 1, RANK, kv_local)
    (grad_in,) = call(
        final_kernel,
        "final",
        [((n_rows, features), BF16)],
        (after, up, down, first, second, from_below, from_above, last_below, last_above),
    )
    return grad_in.reshape(1, micro_count, tok_local, features), grad_down, grad_up


def solution(mesh):
    in_specs = (
        P("pipe", None, "dp", "tensor"),
        P("pipe", "tensor"),
        P("pipe", "tensor", None),
        P("pipe", None, "tensor", None),
        P("pipe", None, None, None),
        P("pipe", None, "dp", None),
        P(None, "dp"),
        P(),
    )
    out_specs = (
        P("pipe", None, "dp", "tensor"),
        P("pipe", "dp", "tensor", None),
        P("pipe", "dp", None, "tensor"),
    )
    return jax.shard_map(body, mesh=mesh, in_specs=in_specs, out_specs=out_specs, check_vma=False)
```

```python
import functools

import jax
import jax.numpy as jnp
from jax import lax
from jax.experimental import pallas as pl
from jax.experimental.pallas import tpu as pltpu
from jax.sharding import PartitionSpec as P

MODEL_WIDTH = 8192
BLOCK_ROWS = 16
RANK = 64
ADAPTER_SCALE = 2.0
EPS = 1e-06
FIRST_BLOCK = 512
PART_COLUMNS = (256, 1024)
SWAP_COLUMNS = 384
VMEM_LIMIT = 16 * 1024 * 1024
FIRST_VMEM_LIMIT = 62 * 1024 * 1024
NT = (((1,), (1,)), ((), ()))
NN = (((1,), (0,)), ((), ()))
F32 = jnp.float32
BF16 = jnp.bfloat16


def dot(a, b, dims):
    return lax.dot_general(a, b, dims, preferred_element_type=F32)


def first_kernel(
    total_tokens,
    cand_hbm,
    counts_hbm,
    h_hbm,
    gain_hbm,
    weight_hbm,
    shrink_hbm,
    expand_hbm,
    grad_hbm,
    gained_dn_out,
    normed_out,
    scaled_part_out,
    back_out,
    mask_out,
    stat_out,
    gained_dn_ref,
    normed_ref,
    scaled_part_ref,
    back_ref,
    mask_ref,
    stat_ref,
    cand_ref,
    counts_ref,
    h_ref,
    gain_ref,
    weight_ref,
    shrink_ref,
    expand_ref,
    grad_ref,
    scaled_ref,
    sel_ref,
    low_ref,
    sems,
    out_sems,
):
    n_rows, features = h_ref.shape
    n_sel = back_ref.shape[1]
    n_blocks = n_rows // BLOCK_ROWS
    per_micro = cand_ref.shape[1]
    n_cand = counts_ref.shape[0]
    kv_local = scaled_part_ref.shape[1]
    fb = FIRST_BLOCK
    n_steps = features // fb
    pairs = [
        (cand_hbm, cand_ref),
        (counts_hbm, counts_ref),
        (grad_hbm, grad_ref),
        (expand_hbm, expand_ref),
        (h_hbm, h_ref),
        (gain_hbm, gain_ref),
        (shrink_hbm, shrink_ref),
    ]
    copies = [
        pltpu.make_async_copy(source, target, sems.at[i]) for i, (source, target) in enumerate(pairs)
    ]
    for step in range(n_steps):
        rows = pl.ds(step * fb, fb)
        copies.append(
            pltpu.make_async_copy(
                weight_hbm.at[rows, :], weight_ref.at[rows, :], sems.at[len(pairs) + step]
            )
        )
    for copy in copies:
        copy.start()
    for copy in copies[:3]:
        copy.wait()

    leaving = []

    def leave(source, target):
        copy = pltpu.make_async_copy(source, target, out_sems.at[len(leaving)])
        copy.start()
        leaving.append(copy)

    owner = lax.broadcasted_iota(jnp.int32, (BLOCK_ROWS, n_sel), 1) // RANK
    for block in range(n_blocks):
        cand = cand_ref[block // per_micro, block % per_micro]
        count = jnp.full((BLOCK_ROWS, 1), counts_ref[cand], jnp.int32).astype(F32)
        weight = total_tokens / (n_cand * count)
        rows = pl.ds(block * BLOCK_ROWS, BLOCK_ROWS)
        scaled_ref[rows, :] = (grad_ref[rows, :].astype(F32) * weight).astype(BF16)
        mask_ref[rows, :] = jnp.where(owner == cand, 1.0, 0.0).astype(BF16)
    first_column = pl.multiple_of(lax.axis_index("tensor") * kv_local, kv_local)
    scaled_part_ref[...] = scaled_ref[:, pl.ds(first_column, kv_local)]
    leave(scaled_part_ref, scaled_part_out)
    leave(mask_ref, mask_out)
    copies[3].wait()
    back = dot(scaled_ref[...], expand_ref[...], NT) * mask_ref[...].astype(F32)
    back_ref[...] = back
    leave(back_ref, back_out)
    sel_ref[...] = back.astype(BF16)
    copies[4].wait()
    copies[5].wait()
    copies[6].wait()

    sumsq = jnp.zeros((n_rows, 1), F32)
    proj = jnp.zeros((n_rows, 1), F32)
    for step in range(n_steps):
        columns = pl.ds(step * fb, fb)
        h16 = h_ref[:, columns]
        h = h16.astype(F32)
        gain = gain_ref[:, columns]
        gained = h * gain
        normed = gained.astype(BF16)
        normed_ref[:, columns] = normed
        leave(normed_ref.at[:, columns], normed_out.at[:, columns])
        shrink = shrink_ref[:, columns]
        low = dot(normed, shrink, NT)
        if step == 0:
            low_ref[...] = low
        else:
            low_ref[...] += low
        sumsq += jnp.sum(h * h, axis=1, keepdims=True)
        adapter = dot(sel_ref[...], shrink, NN)
        copies[len(pairs) + step].wait()
        dn = dot(scaled_ref[...], weight_ref[columns, :], NT) + ADAPTER_SCALE * adapter
        gained_dn_ref[:, columns] = gain * dn
        leave(gained_dn_ref.at[:, columns], gained_dn_out.at[:, columns])
        proj += jnp.sum(gained * dn, axis=1, keepdims=True)

    masked = low_ref[...] * mask_ref[...].astype(F32)
    folded = masked[:, : 2 * RANK]
    for part in range(1, n_sel // (2 * RANK)):
        folded += masked[:, part * 2 * RANK : (part + 1) * 2 * RANK]
    folded += pltpu.roll(folded, RANK, 1)
    lane = lax.broadcasted_iota(jnp.int32, (n_rows, 2 * RANK), 1)
    stat_ref[...] = jnp.where(
        lane < RANK,
        folded,
        jnp.where(lane == RANK, sumsq, jnp.where(lane == RANK + 1, proj, 0.0)),
    )
    leave(stat_ref, stat_out)
    for copy in leaving:
        copy.wait()


def quarters():
    odd = lax.rem(lax.axis_index("pipe"), 2)
    return odd, (1 + 2 * odd, 2 - 2 * odd, odd, 3 - odd)


def rows_of(quarter, size):
    return pl.ds(pl.multiple_of(quarter * size, size), size)


def contrib_kernel(
    here_ref,
    there_ref,
    gained_dn_ref,
    h_hbm,
    up_ref,
    down_ref,
    first_ref,
    second_ref,
    h_ref,
    sems,
):
    size = up_ref.shape[0]
    order = quarters()[1]
    loads = []
    for i, quarter in enumerate(order):
        rows = rows_of(quarter, size)
        loads.append(pltpu.make_async_copy(h_hbm.at[rows, :], h_ref.at[rows, :], sems.at[i]))
    for copy in loads:
        copy.start()
    for i, target in enumerate((up_ref, down_ref, first_ref, second_ref)):
        rows = rows_of(order[i], size)
        stat = here_ref[rows, :] + there_ref[rows, :]
        rms = jnp.sqrt(stat[:, RANK : RANK + 1] / MODEL_WIDTH + EPS)
        inv = 1.0 / rms
        proj = stat[:, RANK + 1 : RANK + 2] / (MODEL_WIDTH * rms * rms * rms)
        loads[i].wait()
        target[...] = gained_dn_ref[rows, :] * inv - h_ref[rows, :].astype(F32) * proj


def pair_kernel(first_ref, second_ref, from_below_ref, from_above_ref, pair_ref):
    section = lax.axis_index("pipe")
    last = lax.axis_size("pipe") - 1
    odd = lax.rem(section, 2)
    owners, rows2, _ = pair_ref.shape
    rows = rows2 // 2
    for owner in range(owners):
        part = pl.ds(owner * rows, rows)
        below = from_below_ref[part, :]
        above = from_above_ref[part, :]
        pair_ref[owner, :rows, :] = first_ref[part, :] + jnp.where(odd == 1, below, above)
        mine = jnp.where(section == 0, 0.0, second_ref[part, :])
        other = jnp.where(odd == 1, above, below)
        pair_ref[owner, rows:, :] = mine + jnp.where(section == last, 0.0, other)


def scan_kernel(owned_ref, after_ref):
    groups, rows2, _ = owned_ref.shape
    rows = rows2 // 2
    total = jnp.zeros((rows, owned_ref.shape[2]), F32)
    for group in range(groups - 1, -1, -1):
        after_ref[group, :rows, :] = total
        if group:
            total = total + owned_ref[group, :rows, :]
    shift = 1 - lax.rem(lax.axis_index("pipe"), 2)
    places = [lax.rem(group + shift, groups) for group in range(groups)]
    total = owned_ref[places[groups - 1], rows:, :]
    for group in range(groups - 2, -1, -1):
        after_ref[places[group], rows:, :] = total
        total = total + owned_ref[places[group], rows:, :]
    after_ref[places[groups - 1], rows:, :] = total


def spread_kernel(after_ref, first_ref, second_ref, up_ref, down_ref):
    section = lax.axis_index("pipe")
    odd = lax.rem(section, 2)
    owners, rows2, _ = after_ref.shape
    rows = rows2 // 2
    for owner in range(owners):
        part = pl.ds(owner * rows, rows)
        after_first = after_ref[owner, :rows, :]
        after_second = after_ref[owner, rows:, :]
        up_ref[part, :] = jnp.where(odd == 1, after_second, after_first)
        down = jnp.where(
            odd == 1, after_first + first_ref[part, :], after_second + second_ref[part, :]
        )
        down_ref[part, :] = jnp.where(section == 0, 0.0, down)


def final_kernel(
    after_ref,
    up_ref,
    down_ref,
    first_ref,
    second_ref,
    from_below_ref,
    from_above_ref,
    last_below_ref,
    last_above_ref,
    out_ref,
):
    section = lax.axis_index("pipe")
    last = lax.axis_size("pipe") - 1
    odd, (up, down, first, second) = quarters()
    owners, rows2, _ = after_ref.shape
    rows = rows2 // 2
    size = owners * rows
    for owner in range(owners):
        part = pl.ds(owner * rows, rows)

        def place(quarter):
            return pl.ds(pl.multiple_of(quarter * size + owner * rows, rows), rows)

        above = from_above_ref[part, :]
        after = after_ref[owner, :rows, :] + jnp.where(odd == 1, 0.0, above)
        out_ref[place(first), :] = (after + first_ref[part, :]).astype(BF16)
        after = after_ref[owner, rows:, :] + jnp.where(odd == 1, above, 0.0)
        after = jnp.where(section == last, 0.0, after)
        out_ref[place(second), :] = (after + second_ref[part, :]).astype(BF16)
        out_ref[place(up), :] = (last_above_ref[part, :] + up_ref[part, :]).astype(BF16)
        out_ref[place(down), :] = (last_below_ref[part, :] + down_ref[part, :]).astype(BF16)


def adapter_kernel(
    here_ref,
    there_ref,
    back_ref,
    mask_ref,
    normed_ref,
    scaled_ref,
    *refs,
):
    *parts, norm_sel_ref, low_sel_ref = refs
    n_parts = len(PART_COLUMNS) + 1
    swaps = parts[2 * n_parts :]
    ring = len(swaps)
    n_rows, n_sel = back_ref.shape
    features = normed_ref.shape[1]
    half = n_sel // 2
    stat = here_ref[...] + there_ref[...]
    rms = jnp.sqrt(stat[:, RANK : RANK + 1] / MODEL_WIDTH + EPS)
    norm_sel_ref[...] = (back_ref[...] / rms).T.astype(BF16)
    lane = lax.broadcasted_iota(jnp.int32, (n_rows, 2 * RANK), 1)
    low = jnp.where(lane < RANK, stat / rms, 0.0)
    low = low + pltpu.roll(low, RANK, 1)
    low = jnp.concatenate([low] * (n_sel // (2 * RANK)), axis=1)
    low_sel_ref[...] = (low * mask_ref[...].astype(F32)).T.astype(BF16)
    mine = lax.axis_index("dp") // ring
    for targets, part in ((parts[n_parts : 2 * n_parts], 1 - mine), (parts[:n_parts], mine)):
        rows = rows_of(part, half)
        norm_sel = norm_sel_ref[rows, :]
        start = 0
        for i, target in enumerate(targets):
            if i == n_parts - 1:
                start += SWAP_COLUMNS
            width = min(target.shape[1], features - start)
            for offset in range(0, width, FIRST_BLOCK):
                size = min(FIRST_BLOCK, width - offset)
                normed = normed_ref[:, start + offset : start + offset + size]
                target[:, offset : offset + size] = ADAPTER_SCALE * dot(norm_sel, normed, NN)
            start += width
            if width < target.shape[1]:
                target[:, width:] = ADAPTER_SCALE * dot(low_sel_ref[rows, :], scaled_ref[...], NN)
    start = sum(PART_COLUMNS)
    normed = normed_ref[:, start : start + SWAP_COLUMNS]
    mine = lax.rem(lax.axis_index("dp"), ring)
    for shift, target in enumerate(swaps):
        owner = lax.rem(mine + shift, ring)
        for upper in range(2):
            norm_sel = norm_sel_ref[rows_of(upper * ring + owner, RANK), :]
            target[upper * RANK : (upper + 1) * RANK, :] = ADAPTER_SCALE * dot(norm_sel, normed, NN)


def split_kernel(keep_ref, come_ref, own_ref, *send_refs):
    parts = keep_ref.shape[0] // RANK
    mine = lax.rem(lax.axis_index("dp"), parts)
    for shift, target in enumerate((own_ref, *send_refs)):
        rows = rows_of(lax.rem(mine + shift, parts), RANK)
        target[...] = keep_ref[rows, :] + come_ref[rows, :]


def sum_kernel(*refs):
    total = refs[0][...]
    for ref in refs[1:-1]:
        total = total + ref[...]
    refs[-1][...] = total


def swap_kernel(*refs):
    *shares, keep_ref, send_ref, total_ref = refs
    total = shares[0][...]
    for ref in shares[1:]:
        total = total + ref[...]
    total_ref[...] = total
    mine = lax.axis_index("dp") // len(shares)
    keep_ref[...] = total_ref[rows_of(mine, RANK), :]
    send_ref[...] = total_ref[rows_of(1 - mine, RANK), :]


def gather_kernel(part_0_ref, part_1_ref, swap_keep_ref, swap_come_ref, *refs):
    *shares, down_ref, up_ref = refs
    total = shares[0][...]
    for ref in shares[1:]:
        total = total + ref[...]
    start = 0
    for value in (part_0_ref[...], part_1_ref[...], swap_keep_ref[...] + swap_come_ref[...]):
        down_ref[:, start : start + value.shape[1]] = value
        start += value.shape[1]
    width = down_ref.shape[1] - start
    down_ref[:, start:] = total[:, :width]
    up_ref[...] = total[:, width:]


def call(kernel, name, outs, args, far=(), far_outs=(), scratch=(), limit=VMEM_LIMIT):
    def spec(place, places):
        return pl.BlockSpec(memory_space=pltpu.HBM if place in places else pltpu.VMEM)

    return pl.pallas_call(
        kernel,
        in_specs=[spec(i, far) for i in range(len(args))],
        out_specs=[spec(i, far_outs) for i in range(len(outs))],
        out_shape=[jax.ShapeDtypeStruct(shape, kind) for shape, kind in outs],
        scratch_shapes=list(scratch),
        compiler_params=pltpu.CompilerParams(vmem_limit_bytes=limit),
        name=name,
    )(*args)


def body(
    norm_input,
    gain,
    value_weight,
    shrink_factor_matrices,
    expand_factor_matrices,
    value_gradient,
    candidate_index,
    counts,
):
    micro_count, tok_local, features = norm_input.shape[1:]
    n_rows = micro_count * tok_local
    n_cand = counts.shape[0]
    kv_width = value_weight.shape[2]
    n_tensor = lax.axis_size("tensor")
    n_pipe = lax.axis_size("pipe")
    n_dp = lax.axis_size("dp")
    kv_local = kv_width // n_tensor
    n_sel = n_cand * RANK
    wide = features + kv_local
    total_tokens = float(n_rows * n_dp)
    h = norm_input.reshape(n_rows, features)
    shrink = shrink_factor_matrices[0].transpose(0, 2, 1).reshape(n_sel, features)
    expand = expand_factor_matrices.reshape(n_sel, kv_width)
    gradient = value_gradient.reshape(n_rows, kv_width)

    outs = [
        ((n_rows, features), F32),
        ((n_rows, features), BF16),
        ((n_rows, kv_local), BF16),
        ((n_rows, n_sel), F32),
        ((n_rows, n_sel), BF16),
        ((n_rows, 2 * RANK), F32),
    ]
    gained_dn, normed, scaled_part, back, mask, stat = call(
        functools.partial(first_kernel, total_tokens),
        "first",
        outs,
        (candidate_index, counts, h, gain, value_weight[0], shrink, expand, gradient),
        far=range(8),
        far_outs=range(6),
        limit=FIRST_VMEM_LIMIT,
        scratch=[pltpu.VMEM(shape, kind) for shape, kind in outs]
        + [
            pltpu.SMEM(candidate_index.shape, jnp.int32),
            pltpu.SMEM(counts.shape, jnp.int32),
            pltpu.VMEM((n_rows, features), BF16),
            pltpu.VMEM((1, features), F32),
            pltpu.VMEM((features, kv_width), BF16),
            pltpu.VMEM((n_sel, features), BF16),
            pltpu.VMEM((n_sel, kv_width), BF16),
            pltpu.VMEM((n_rows, kv_width), BF16),
            pltpu.VMEM((n_rows, kv_width), BF16),
            pltpu.VMEM((n_rows, n_sel), BF16),
            pltpu.VMEM((n_rows, n_sel), F32),
            pltpu.SemaphoreType.DMA((7 + features // FIRST_BLOCK,)),
            pltpu.SemaphoreType.DMA((4 + 2 * (features // FIRST_BLOCK),)),
        ],
    )

    near = [(i, i ^ 1) for i in range(n_tensor)]
    far = [(i, (i + n_tensor // 2) % n_tensor) for i in range(n_tensor)]
    here = stat + lax.ppermute(stat, "tensor", near)
    there = lax.ppermute(here, "tensor", far)

    quarter = (n_rows // 4, features)
    up, down, first, second = call(
        contrib_kernel,
        "contrib",
        [(quarter, F32)] * 4,
        (here, there, gained_dn, h),
        far=(3,),
        scratch=[pltpu.VMEM((n_rows, features), BF16), pltpu.SemaphoreType.DMA((4,))],
    )
    rise = [(i, (i + 1) % n_pipe) for i in range(n_pipe)]
    fall = [(i, (i - 1) % n_pipe) for i in range(n_pipe)]
    from_below = lax.ppermute(up, "pipe", rise)
    from_above = lax.ppermute(down, "pipe", fall)

    half = n_sel // 2
    ring = n_dp // 2
    widths = (*PART_COLUMNS, wide - sum(PART_COLUMNS) - SWAP_COLUMNS)
    n_parts = len(widths)
    adapter = call(
        adapter_kernel,
        "adapter",
        [((half, width), F32) for width in widths] * 2 + [((2 * RANK, SWAP_COLUMNS), F32)] * ring,
        (here, there, back, mask, normed, scaled_part),
        scratch=[pltpu.VMEM((n_sel, n_rows), BF16)] * 2,
    )
    keep, send = adapter[:n_parts], list(adapter[n_parts : 2 * n_parts])
    swaps = adapter[2 * n_parts :]

    def over(value):
        pairs = [(i, (i + ring) % n_dp) for i in range(n_dp)]
        return lax.ppermute(value, "dp", pairs)

    def across(part):
        return over(send[part])

    def around(part, came):
        out = [((RANK, widths[part]), F32)] * ring
        return turned(call(split_kernel, "split", out, (keep[part], came)))

    def turned(values):
        own, *sends = values
        shares = [own]
        for shift, value in enumerate(sends, 1):
            pairs = [(i, i // ring * ring + (i + shift) % ring) for i in range(n_dp)]
            shares.append(lax.ppermute(value, "dp", pairs))
        return shares

    def summed(part, shares):
        return call(sum_kernel, "sum", [((RANK, widths[part]), F32)], shares)[0]

    groups = n_pipe // 2
    lines = [list(range(first, n_pipe, 2)) for first in range(2)]
    shape = (groups, n_rows // 2 // groups, features)
    came = across(0)
    from_below, from_above, came, send[1], send[2], *swaps = lax.optimization_barrier(
        (from_below, from_above, came, send[1], send[2], *swaps)
    )
    (pair,) = call(pair_kernel, "pair", [(shape, F32)], (first, second, from_below, from_above))
    owned = lax.all_to_all(pair, "pipe", 0, 0, axis_index_groups=lines, tiled=True)
    part_0 = summed(0, around(0, came))
    came = across(1)
    swap_keep, swap_send = call(
        swap_kernel,
        "swap",
        [((RANK, SWAP_COLUMNS), F32)] * 2,
        turned(swaps),
        scratch=[pltpu.VMEM((2 * RANK, SWAP_COLUMNS), F32)],
    )
    owned, part_0, came, send[2], swap_send = lax.optimization_barrier(
        (owned, part_0, came, send[2], swap_send)
    )
    (after,) = call(scan_kernel, "scan", [(shape, F32)], (owned,))
    after = lax.all_to_all(after, "pipe", 0, 0, axis_index_groups=lines, tiled=True)
    part_1 = summed(1, around(1, came))
    came = across(2)
    swap_come = over(swap_send)
    after, part_1, came, swap_come = lax.optimization_barrier((after, part_1, came, swap_come))
    shares = around(2, came)
    rising, falling = call(spread_kernel, "spread", [(quarter, F32)] * 2, (after, first, second))
    last_below = lax.ppermute(rising, "pipe", rise)
    last_above = lax.ppermute(falling, "pipe", fall)
    grad_down, grad_up = call(
        gather_kernel, "gather", [((RANK, features), F32), ((RANK, kv_local), F32)], [part_0, part_1, swap_keep, swap_come, *shares]
    )
    grad_down = grad_down.reshape(1, 1, RANK, features).transpose(0, 1, 3, 2)
    grad_up = grad_up.reshape(1, 1, RANK, kv_local)
    (grad_in,) = call(
        final_kernel,
        "final",
        [((n_rows, features), BF16)],
        (after, up, down, first, second, from_below, from_above, last_below, last_above),
    )
    return grad_in.reshape(1, micro_count, tok_local, features), grad_down, grad_up


def solution(mesh):
    in_specs = (
        P("pipe", None, "dp", "tensor"),
        P("pipe", "tensor"),
        P("pipe", "tensor", None),
        P("pipe", None, "tensor", None),
        P("pipe", None, None, None),
        P("pipe", None, "dp", None),
        P(None, "dp"),
        P(),
    )
    out_specs = (
        P("pipe", None, "dp", "tensor"),
        P("pipe", "dp", "tensor", None),
        P("pipe", "dp", None, "tensor"),
    )
    return jax.shard_map(body, mesh=mesh, in_specs=in_specs, out_specs=out_specs, check_vma=False)
```

```python
import functools

import jax
import jax.numpy as jnp
from jax import lax
from jax.experimental import pallas as pl
from jax.experimental.pallas import tpu as pltpu
from jax.sharding import PartitionSpec as P

MODEL_WIDTH = 8192
BLOCK_ROWS = 16
RANK = 64
ADAPTER_SCALE = 2.0
EPS = 1e-06
FIRST_BLOCK = 256
PART_COLUMNS = (256, 1024)
SWAP_COLUMNS = 384
VMEM_LIMIT = 16 * 1024 * 1024
FIRST_VMEM_LIMIT = 62 * 1024 * 1024
NT = (((1,), (1,)), ((), ()))
NN = (((1,), (0,)), ((), ()))
F32 = jnp.float32
BF16 = jnp.bfloat16


def dot(a, b, dims):
    return lax.dot_general(a, b, dims, preferred_element_type=F32)


def first_kernel(
    total_tokens,
    cand_hbm,
    counts_hbm,
    h_hbm,
    gain_hbm,
    weight_hbm,
    shrink_hbm,
    expand_hbm,
    grad_hbm,
    gained_dn_out,
    normed_out,
    scaled_part_out,
    back_out,
    mask_out,
    stat_out,
    gained_dn_ref,
    normed_ref,
    scaled_part_ref,
    back_ref,
    mask_ref,
    stat_ref,
    cand_ref,
    counts_ref,
    h_ref,
    gain_ref,
    weight_ref,
    shrink_ref,
    expand_ref,
    grad_ref,
    scaled_ref,
    sel_ref,
    low_ref,
    sems,
    out_sems,
):
    n_rows, features = h_ref.shape
    n_sel = back_ref.shape[1]
    n_blocks = n_rows // BLOCK_ROWS
    per_micro = cand_ref.shape[1]
    n_cand = counts_ref.shape[0]
    kv_local = scaled_part_ref.shape[1]
    fb = FIRST_BLOCK
    n_steps = features // fb
    pairs = [
        (cand_hbm, cand_ref),
        (counts_hbm, counts_ref),
        (grad_hbm, grad_ref),
        (expand_hbm, expand_ref),
        (h_hbm, h_ref),
        (gain_hbm, gain_ref),
        (shrink_hbm, shrink_ref),
    ]
    copies = [
        pltpu.make_async_copy(source, target, sems.at[i]) for i, (source, target) in enumerate(pairs)
    ]
    for step in range(n_steps):
        rows = pl.ds(step * fb, fb)
        copies.append(
            pltpu.make_async_copy(
                weight_hbm.at[rows, :], weight_ref.at[rows, :], sems.at[len(pairs) + step]
            )
        )
    for copy in copies:
        copy.start()
    for copy in copies[:3]:
        copy.wait()

    leaving = []

    def leave(source, target):
        copy = pltpu.make_async_copy(source, target, out_sems.at[len(leaving)])
        copy.start()
        leaving.append(copy)

    owner = lax.broadcasted_iota(jnp.int32, (BLOCK_ROWS, n_sel), 1) // RANK
    for block in range(n_blocks):
        cand = cand_ref[block // per_micro, block % per_micro]
        count = jnp.full((BLOCK_ROWS, 1), counts_ref[cand], jnp.int32).astype(F32)
        weight = total_tokens / (n_cand * count)
        rows = pl.ds(block * BLOCK_ROWS, BLOCK_ROWS)
        scaled_ref[rows, :] = (grad_ref[rows, :].astype(F32) * weight).astype(BF16)
        mask_ref[rows, :] = jnp.where(owner == cand, 1.0, 0.0).astype(BF16)
    first_column = pl.multiple_of(lax.axis_index("tensor") * kv_local, kv_local)
    scaled_part_ref[...] = scaled_ref[:, pl.ds(first_column, kv_local)]
    leave(scaled_part_ref, scaled_part_out)
    leave(mask_ref, mask_out)
    copies[3].wait()
    back = dot(scaled_ref[...], expand_ref[...], NT) * mask_ref[...].astype(F32)
    back_ref[...] = back
    leave(back_ref, back_out)
    sel_ref[...] = back.astype(BF16)
    copies[4].wait()
    copies[5].wait()
    copies[6].wait()

    sumsq = jnp.zeros((n_rows, 1), F32)
    proj = jnp.zeros((n_rows, 1), F32)
    for step in range(n_steps):
        columns = pl.ds(step * fb, fb)
        h16 = h_ref[:, columns]
        h = h16.astype(F32)
        gain = gain_ref[:, columns]
        gained = h * gain
        normed = gained.astype(BF16)
        normed_ref[:, columns] = normed
        leave(normed_ref.at[:, columns], normed_out.at[:, columns])
        shrink = shrink_ref[:, columns]
        low = dot(normed, shrink, NT)
        if step == 0:
            low_ref[...] = low
        else:
            low_ref[...] += low
        sumsq += jnp.sum(h * h, axis=1, keepdims=True)
        adapter = dot(sel_ref[...], shrink, NN)
        copies[len(pairs) + step].wait()
        dn = dot(scaled_ref[...], weight_ref[columns, :], NT) + ADAPTER_SCALE * adapter
        gained_dn_ref[:, columns] = gain * dn
        leave(gained_dn_ref.at[:, columns], gained_dn_out.at[:, columns])
        proj += jnp.sum(gained * dn, axis=1, keepdims=True)

    masked = low_ref[...] * mask_ref[...].astype(F32)
    folded = masked[:, : 2 * RANK]
    for part in range(1, n_sel // (2 * RANK)):
        folded += masked[:, part * 2 * RANK : (part + 1) * 2 * RANK]
    folded += pltpu.roll(folded, RANK, 1)
    lane = lax.broadcasted_iota(jnp.int32, (n_rows, 2 * RANK), 1)
    stat_ref[...] = jnp.where(
        lane < RANK,
        folded,
        jnp.where(lane == RANK, sumsq, jnp.where(lane == RANK + 1, proj, 0.0)),
    )
    leave(stat_ref, stat_out)
    for copy in leaving:
        copy.wait()


def quarters():
    odd = lax.rem(lax.axis_index("pipe"), 2)
    return odd, (1 + 2 * odd, 2 - 2 * odd, odd, 3 - odd)


def rows_of(quarter, size):
    return pl.ds(pl.multiple_of(quarter * size, size), size)


def contrib_kernel(
    here_ref,
    there_ref,
    gained_dn_ref,
    h_hbm,
    up_ref,
    down_ref,
    first_ref,
    second_ref,
    h_ref,
    sems,
):
    size = up_ref.shape[0]
    order = quarters()[1]
    loads = []
    for i, quarter in enumerate(order):
        rows = rows_of(quarter, size)
        loads.append(pltpu.make_async_copy(h_hbm.at[rows, :], h_ref.at[rows, :], sems.at[i]))
    for copy in loads:
        copy.start()
    for i, target in enumerate((up_ref, down_ref, first_ref, second_ref)):
        rows = rows_of(order[i], size)
        stat = here_ref[rows, :] + there_ref[rows, :]
        rms = jnp.sqrt(stat[:, RANK : RANK + 1] / MODEL_WIDTH + EPS)
        inv = 1.0 / rms
        proj = stat[:, RANK + 1 : RANK + 2] / (MODEL_WIDTH * rms * rms * rms)
        loads[i].wait()
        target[...] = gained_dn_ref[rows, :] * inv - h_ref[rows, :].astype(F32) * proj


def pair_kernel(first_ref, second_ref, from_below_ref, from_above_ref, pair_ref):
    section = lax.axis_index("pipe")
    last = lax.axis_size("pipe") - 1
    odd = lax.rem(section, 2)
    owners, rows2, _ = pair_ref.shape
    rows = rows2 // 2
    for owner in range(owners):
        part = pl.ds(owner * rows, rows)
        below = from_below_ref[part, :]
        above = from_above_ref[part, :]
        pair_ref[owner, :rows, :] = first_ref[part, :] + jnp.where(odd == 1, below, above)
        mine = jnp.where(section == 0, 0.0, second_ref[part, :])
        other = jnp.where(odd == 1, above, below)
        pair_ref[owner, rows:, :] = mine + jnp.where(section == last, 0.0, other)


def scan_kernel(owned_ref, after_ref):
    groups, rows2, _ = owned_ref.shape
    rows = rows2 // 2
    total = jnp.zeros((rows, owned_ref.shape[2]), F32)
    for group in range(groups - 1, -1, -1):
        after_ref[group, :rows, :] = total
        if group:
            total = total + owned_ref[group, :rows, :]
    shift = 1 - lax.rem(lax.axis_index("pipe"), 2)
    places = [lax.rem(group + shift, groups) for group in range(groups)]
    total = owned_ref[places[groups - 1], rows:, :]
    for group in range(groups - 2, -1, -1):
        after_ref[places[group], rows:, :] = total
        total = total + owned_ref[places[group], rows:, :]
    after_ref[places[groups - 1], rows:, :] = total


def spread_kernel(after_ref, first_ref, second_ref, up_ref, down_ref):
    section = lax.axis_index("pipe")
    odd = lax.rem(section, 2)
    owners, rows2, _ = after_ref.shape
    rows = rows2 // 2
    for owner in range(owners):
        part = pl.ds(owner * rows, rows)
        after_first = after_ref[owner, :rows, :]
        after_second = after_ref[owner, rows:, :]
        up_ref[part, :] = jnp.where(odd == 1, after_second, after_first)
        down = jnp.where(
            odd == 1, after_first + first_ref[part, :], after_second + second_ref[part, :]
        )
        down_ref[part, :] = jnp.where(section == 0, 0.0, down)


def final_kernel(
    after_ref,
    up_ref,
    down_ref,
    first_ref,
    second_ref,
    from_below_ref,
    from_above_ref,
    last_below_ref,
    last_above_ref,
    out_ref,
):
    section = lax.axis_index("pipe")
    last = lax.axis_size("pipe") - 1
    odd, (up, down, first, second) = quarters()
    owners, rows2, _ = after_ref.shape
    rows = rows2 // 2
    size = owners * rows
    for owner in range(owners):
        part = pl.ds(owner * rows, rows)

        def place(quarter):
            return pl.ds(pl.multiple_of(quarter * size + owner * rows, rows), rows)

        above = from_above_ref[part, :]
        after = after_ref[owner, :rows, :] + jnp.where(odd == 1, 0.0, above)
        out_ref[place(first), :] = (after + first_ref[part, :]).astype(BF16)
        after = after_ref[owner, rows:, :] + jnp.where(odd == 1, above, 0.0)
        after = jnp.where(section == last, 0.0, after)
        out_ref[place(second), :] = (after + second_ref[part, :]).astype(BF16)
        out_ref[place(up), :] = (last_above_ref[part, :] + up_ref[part, :]).astype(BF16)
        out_ref[place(down), :] = (last_below_ref[part, :] + down_ref[part, :]).astype(BF16)


def adapter_kernel(
    here_ref,
    there_ref,
    back_ref,
    mask_ref,
    normed_ref,
    scaled_ref,
    *refs,
):
    *parts, norm_sel_ref, low_sel_ref = refs
    n_parts = len(PART_COLUMNS) + 1
    swaps = parts[2 * n_parts :]
    ring = len(swaps)
    n_rows, n_sel = back_ref.shape
    features = normed_ref.shape[1]
    half = n_sel // 2
    stat = here_ref[...] + there_ref[...]
    rms = jnp.sqrt(stat[:, RANK : RANK + 1] / MODEL_WIDTH + EPS)
    norm_sel_ref[...] = (back_ref[...] / rms).T.astype(BF16)
    lane = lax.broadcasted_iota(jnp.int32, (n_rows, 2 * RANK), 1)
    low = jnp.where(lane < RANK, stat / rms, 0.0)
    low = low + pltpu.roll(low, RANK, 1)
    low = jnp.concatenate([low] * (n_sel // (2 * RANK)), axis=1)
    low_sel_ref[...] = (low * mask_ref[...].astype(F32)).T.astype(BF16)
    mine = lax.axis_index("dp") // ring
    for targets, part in ((parts[n_parts : 2 * n_parts], 1 - mine), (parts[:n_parts], mine)):
        rows = rows_of(part, half)
        norm_sel = norm_sel_ref[rows, :]
        start = 0
        for i, target in enumerate(targets):
            if i == n_parts - 1:
                start += SWAP_COLUMNS
            width = min(target.shape[1], features - start)
            for offset in range(0, width, FIRST_BLOCK):
                size = min(FIRST_BLOCK, width - offset)
                normed = normed_ref[:, start + offset : start + offset + size]
                target[:, offset : offset + size] = ADAPTER_SCALE * dot(norm_sel, normed, NN)
            start += width
            if width < target.shape[1]:
                target[:, width:] = ADAPTER_SCALE * dot(low_sel_ref[rows, :], scaled_ref[...], NN)
    start = sum(PART_COLUMNS)
    normed = normed_ref[:, start : start + SWAP_COLUMNS]
    mine = lax.rem(lax.axis_index("dp"), ring)
    for shift, target in enumerate(swaps):
        owner = lax.rem(mine + shift, ring)
        for upper in range(2):
            norm_sel = norm_sel_ref[rows_of(upper * ring + owner, RANK), :]
            target[upper * RANK : (upper + 1) * RANK, :] = ADAPTER_SCALE * dot(norm_sel, normed, NN)


def split_kernel(keep_ref, come_ref, own_ref, *send_refs):
    parts = keep_ref.shape[0] // RANK
    mine = lax.rem(lax.axis_index("dp"), parts)
    for shift, target in enumerate((own_ref, *send_refs)):
        rows = rows_of(lax.rem(mine + shift, parts), RANK)
        target[...] = keep_ref[rows, :] + come_ref[rows, :]


def sum_kernel(*refs):
    total = refs[0][...]
    for ref in refs[1:-1]:
        total = total + ref[...]
    refs[-1][...] = total


def swap_kernel(*refs):
    *shares, keep_ref, send_ref, total_ref = refs
    total = shares[0][...]
    for ref in shares[1:]:
        total = total + ref[...]
    total_ref[...] = total
    mine = lax.axis_index("dp") // len(shares)
    keep_ref[...] = total_ref[rows_of(mine, RANK), :]
    send_ref[...] = total_ref[rows_of(1 - mine, RANK), :]


def gather_kernel(part_0_ref, part_1_ref, swap_keep_ref, swap_come_ref, *refs):
    *shares, down_ref, up_ref = refs
    total = shares[0][...]
    for ref in shares[1:]:
        total = total + ref[...]
    start = 0
    for value in (part_0_ref[...], part_1_ref[...], swap_keep_ref[...] + swap_come_ref[...]):
        down_ref[:, start : start + value.shape[1]] = value
        start += value.shape[1]
    width = down_ref.shape[1] - start
    down_ref[:, start:] = total[:, :width]
    up_ref[...] = total[:, width:]


def call(kernel, name, outs, args, far=(), far_outs=(), scratch=(), limit=VMEM_LIMIT):
    def spec(place, places):
        return pl.BlockSpec(memory_space=pltpu.HBM if place in places else pltpu.VMEM)

    return pl.pallas_call(
        kernel,
        in_specs=[spec(i, far) for i in range(len(args))],
        out_specs=[spec(i, far_outs) for i in range(len(outs))],
        out_shape=[jax.ShapeDtypeStruct(shape, kind) for shape, kind in outs],
        scratch_shapes=list(scratch),
        compiler_params=pltpu.CompilerParams(vmem_limit_bytes=limit),
        name=name,
    )(*args)


def body(
    norm_input,
    gain,
    value_weight,
    shrink_factor_matrices,
    expand_factor_matrices,
    value_gradient,
    candidate_index,
    counts,
):
    micro_count, tok_local, features = norm_input.shape[1:]
    n_rows = micro_count * tok_local
    n_cand = counts.shape[0]
    kv_width = value_weight.shape[2]
    n_tensor = lax.axis_size("tensor")
    n_pipe = lax.axis_size("pipe")
    n_dp = lax.axis_size("dp")
    kv_local = kv_width // n_tensor
    n_sel = n_cand * RANK
    wide = features + kv_local
    total_tokens = float(n_rows * n_dp)
    h = norm_input.reshape(n_rows, features)
    shrink = shrink_factor_matrices[0].transpose(0, 2, 1).reshape(n_sel, features)
    expand = expand_factor_matrices.reshape(n_sel, kv_width)
    gradient = value_gradient.reshape(n_rows, kv_width)

    outs = [
        ((n_rows, features), F32),
        ((n_rows, features), BF16),
        ((n_rows, kv_local), BF16),
        ((n_rows, n_sel), F32),
        ((n_rows, n_sel), BF16),
        ((n_rows, 2 * RANK), F32),
    ]
    gained_dn, normed, scaled_part, back, mask, stat = call(
        functools.partial(first_kernel, total_tokens),
        "first",
        outs,
        (candidate_index, counts, h, gain, value_weight[0], shrink, expand, gradient),
        far=range(8),
        far_outs=range(6),
        limit=FIRST_VMEM_LIMIT,
        scratch=[pltpu.VMEM(shape, kind) for shape, kind in outs]
        + [
            pltpu.SMEM(candidate_index.shape, jnp.int32),
            pltpu.SMEM(counts.shape, jnp.int32),
            pltpu.VMEM((n_rows, features), BF16),
            pltpu.VMEM((1, features), F32),
            pltpu.VMEM((features, kv_width), BF16),
            pltpu.VMEM((n_sel, features), BF16),
            pltpu.VMEM((n_sel, kv_width), BF16),
            pltpu.VMEM((n_rows, kv_width), BF16),
            pltpu.VMEM((n_rows, kv_width), BF16),
            pltpu.VMEM((n_rows, n_sel), BF16),
            pltpu.VMEM((n_rows, n_sel), F32),
            pltpu.SemaphoreType.DMA((7 + features // FIRST_BLOCK,)),
            pltpu.SemaphoreType.DMA((4 + 2 * (features // FIRST_BLOCK),)),
        ],
    )

    near = [(i, i ^ 1) for i in range(n_tensor)]
    far = [(i, (i + n_tensor // 2) % n_tensor) for i in range(n_tensor)]
    here = stat + lax.ppermute(stat, "tensor", near)
    there = lax.ppermute(here, "tensor", far)

    quarter = (n_rows // 4, features)
    up, down, first, second = call(
        contrib_kernel,
        "contrib",
        [(quarter, F32)] * 4,
        (here, there, gained_dn, h),
        far=(3,),
        scratch=[pltpu.VMEM((n_rows, features), BF16), pltpu.SemaphoreType.DMA((4,))],
    )
    rise = [(i, (i + 1) % n_pipe) for i in range(n_pipe)]
    fall = [(i, (i - 1) % n_pipe) for i in range(n_pipe)]
    from_below = lax.ppermute(up, "pipe", rise)
    from_above = lax.ppermute(down, "pipe", fall)

    half = n_sel // 2
    ring = n_dp // 2
    widths = (*PART_COLUMNS, wide - sum(PART_COLUMNS) - SWAP_COLUMNS)
    n_parts = len(widths)
    adapter = call(
        adapter_kernel,
        "adapter",
        [((half, width), F32) for width in widths] * 2 + [((2 * RANK, SWAP_COLUMNS), F32)] * ring,
        (here, there, back, mask, normed, scaled_part),
        scratch=[pltpu.VMEM((n_sel, n_rows), BF16)] * 2,
    )
    keep, send = adapter[:n_parts], list(adapter[n_parts : 2 * n_parts])
    swaps = adapter[2 * n_parts :]

    def over(value):
        pairs = [(i, (i + ring) % n_dp) for i in range(n_dp)]
        return lax.ppermute(value, "dp", pairs)

    def across(part):
        return over(send[part])

    def around(part, came):
        out = [((RANK, widths[part]), F32)] * ring
        return turned(call(split_kernel, "split", out, (keep[part], came)))

    def turned(values):
        own, *sends = values
        shares = [own]
        for shift, value in enumerate(sends, 1):
            pairs = [(i, i // ring * ring + (i + shift) % ring) for i in range(n_dp)]
            shares.append(lax.ppermute(value, "dp", pairs))
        return shares

    def summed(part, shares):
        return call(sum_kernel, "sum", [((RANK, widths[part]), F32)], shares)[0]

    groups = n_pipe // 2
    lines = [list(range(first, n_pipe, 2)) for first in range(2)]
    shape = (groups, n_rows // 2 // groups, features)
    came = across(0)
    from_below, from_above, came, send[1], send[2], *swaps = lax.optimization_barrier(
        (from_below, from_above, came, send[1], send[2], *swaps)
    )
    (pair,) = call(pair_kernel, "pair", [(shape, F32)], (first, second, from_below, from_above))
    owned = lax.all_to_all(pair, "pipe", 0, 0, axis_index_groups=lines, tiled=True)
    part_0 = summed(0, around(0, came))
    came = across(1)
    swap_keep, swap_send = call(
        swap_kernel,
        "swap",
        [((RANK, SWAP_COLUMNS), F32)] * 2,
        turned(swaps),
        scratch=[pltpu.VMEM((2 * RANK, SWAP_COLUMNS), F32)],
    )
    owned, part_0, came, send[2], swap_send = lax.optimization_barrier(
        (owned, part_0, came, send[2], swap_send)
    )
    (after,) = call(scan_kernel, "scan", [(shape, F32)], (owned,))
    after = lax.all_to_all(after, "pipe", 0, 0, axis_index_groups=lines, tiled=True)
    part_1 = summed(1, around(1, came))
    came = across(2)
    swap_come = over(swap_send)
    after, part_1, came, swap_come = lax.optimization_barrier((after, part_1, came, swap_come))
    shares = around(2, came)
    rising, falling = call(spread_kernel, "spread", [(quarter, F32)] * 2, (after, first, second))
    last_below = lax.ppermute(rising, "pipe", rise)
    last_above = lax.ppermute(falling, "pipe", fall)
    grad_down, grad_up = call(
        gather_kernel, "gather", [((RANK, features), F32), ((RANK, kv_local), F32)], [part_0, part_1, swap_keep, swap_come, *shares]
    )
    grad_down = grad_down.reshape(1, 1, RANK, features).transpose(0, 1, 3, 2)
    grad_up = grad_up.reshape(1, 1, RANK, kv_local)
    (grad_in,) = call(
        final_kernel,
        "final",
        [((n_rows, features), BF16)],
        (after, up, down, first, second, from_below, from_above, last_below, last_above),
    )
    return grad_in.reshape(1, micro_count, tok_local, features), grad_down, grad_up


def solution(mesh):
    in_specs = (
        P("pipe", None, "dp", "tensor"),
        P("pipe", "tensor"),
        P("pipe", "tensor", None),
        P("pipe", None, "tensor", None),
        P("pipe", None, None, None),
        P("pipe", None, "dp", None),
        P(None, "dp"),
        P(),
    )
    out_specs = (
        P("pipe", None, "dp", "tensor"),
        P("pipe", "dp", "tensor", None),
        P("pipe", "dp", None, "tensor"),
    )
    return jax.shard_map(body, mesh=mesh, in_specs=in_specs, out_specs=out_specs, check_vma=False)
```
